32 devices in a mesh: grp: 2 (over x), dap: 4 (over y, core), sub: 4 (over z).
Axes of the slice: x: 2, y: 2, z: 4, core: 2. Of those that a mesh axis runs over, the one named last changes fastest.
Arguments:
- alignment: bfloat16 [32, 16, 256], P(('grp', 'dap', 'sub')), parts along dimension 0, may hold values from -170 to 170
- pair_bias: bfloat16 [8, 32, 16], P(None, ('grp', 'dap', 'sub')), parts along dimension 1, may hold values from -4 to 250
- row_project: bfloat16 [256, 4, 256], replicated, may hold values from -0.375 to 0.375
- row_output: bfloat16 [256, 256], replicated, may hold values from -0.375 to 0.375
- column_project: bfloat16 [256, 4, 256], replicated, may hold values from -9 to 9
- column_output: bfloat16 [256, 256], replicated, may hold values from -0.375 to 0.375
- transition_in: bfloat16 [256, 2, 1024], replicated, may hold values from -0.375 to 0.375
- transition_out: bfloat16 [1024, 256], replicated, may hold values from -0.1875 to 0.1875
- cotangent: bfloat16 [32, 16, 256], P(('grp', 'dap', 'sub')), parts along dimension 0, may hold values from -6 to 6
Outputs:
- grad_alignment: bfloat16 [32, 16, 256], P(('grp', 'dap', 'sub')), parts along dimension 0
- grad_bias: float32 [8, 32, 16], P(None, ('grp', 'dap', 'sub')), parts along dimension 1
- grad_row_project: float32 [512, 4, 256], P(('grp', 'dap', 'sub')), parts along dimension 0
- grad_row_output: float32 [512, 256], P(('grp', 'dap', 'sub')), parts along dimension 0
- grad_column_project: float32 [512, 4, 256], P(('grp', 'dap', 'sub')), parts along dimension 0
- grad_column_output: float32 [512, 256], P(('grp', 'dap', 'sub')), parts along dimension 0
- grad_transition_in: float32 [512, 2, 1024], P(('grp', 'dap', 'sub')), parts along dimension 0
- grad_transition_out: float32 [2048, 256], P(('grp', 'dap', 'sub')), parts along dimension 0
The draws below stay inside these ranges and needn't reach their ends.
There are 2 independent parts, one for each index of `grp`. The reference program is written for one: setup_inputs(seed, part) draws one part's arguments, and reference() takes and returns one part's arrays. A program takes and returns all parts, laid end to end along the dimension named above; an argument that names none is the same for every part. Nothing has to cross between parts.
All inputs are finite; a program needn't handle non-finite values.
Results may differ from the reference program's by a relative error of at most 0.019.
Values may be sent and summed in bfloat16 or wider, within the bound.
A program may use at most 64 MiB of HBM per device.

```python
import jax
import jax.numpy as jnp
from jax import lax

C = 256
H = 8
DH = 32
FF = 1024
S = 16
R = 16


def draw_alignment(key, part):
    sample = jnp.clip(jax.random.normal(jax.random.fold_in(key, 11), (S, R, C), jnp.float32), -5.0, 5.0)
    return sample.astype(jnp.bfloat16)


def draw_pair_bias(key, part):
    sample = jnp.clip(jax.random.normal(jax.random.fold_in(key, 21), (H, R, R), jnp.float32), -4.0, 4.0)
    return sample.astype(jnp.bfloat16)


def draw_column_project(key, part):
    sample = jnp.clip(jax.random.normal(jax.random.fold_in(key, 31), (C, 4, H * DH), jnp.float32), -6.0, 6.0) * C ** (-0.5)
    return sample.astype(jnp.bfloat16)


def spiked(result, rng, source, target, shards_of, factor):
    owner, partner = [(jnp.arange(result.shape[axis_at]) // (result.shape[axis_at] // shards_of)).reshape([-1 if axis == axis_at else 1 for axis in range(result.ndim)]) for axis_at in (source, target)]
    chosen = jax.random.permutation(rng, shards_of)[partner]
    strong = (owner == chosen) | (owner == (partner + shards_of // 2) % shards_of)
    return jnp.where(strong, factor * result, result)


def level_of(stream_key, shape, cuts, low, largest):
    def one(dim, parts):
        draws = jax.random.uniform(jax.random.fold_in(jax.random.fold_in(stream_key, 6), dim), (parts,), jnp.float32, low / len(cuts), largest / len(cuts))
        return jnp.repeat(jnp.exp(draws), shape[dim] // parts).reshape((-1,) + (1,) * (len(shape) - dim - 1))

    loudness = one(*cuts[0])
    for cut in cuts[1:]:
        loudness = loudness * one(*cut)
    return loudness


def gaussian(own_key, dims, deviation, reach, cuts=(), kind=jnp.bfloat16):
    drawn = jax.random.normal(own_key, dims, jnp.float32) * deviation
    if len(cuts) > 0:
        drawn = level_of(own_key, dims, cuts, -0.22, 0.18) * drawn
    return jnp.clip(drawn, min=-reach, max=reach).astype(kind)


def bell_draw_with(own_key, shape, scale, limit, split, heavy, held_as=jnp.bfloat16):
    entries = scale * jax.random.normal(own_key, shape, jnp.float32)
    if split:
        entries = entries * level_of(own_key, shape, split, -0.22, 0.18)
    return jnp.clip(spiked(entries, jax.random.fold_in(own_key, 3), *heavy), -limit, limit).astype(held_as)


def setup_inputs(seed: int = 0, part: int = 0) -> dict:
    seeds = jax.random.split(jax.random.key(seed), 10)
    part_splits = jax.random.split(jax.random.fold_in(seeds[9], part), 10)
    alignment = draw_alignment(jax.random.fold_in(jax.random.fold_in(seeds[9], part), 71), part)
    pair_bias = draw_pair_bias(jax.random.fold_in(jax.random.fold_in(seeds[9], part), 71), part)
    row_project = gaussian(seeds[2], (C, 4, H * DH), C ** -0.5, 0.375)
    row_output = gaussian(seeds[3], (H * DH, C), (H * DH) ** -0.5, 0.375)
    column_project = draw_column_project(jax.random.fold_in(seeds[9], 71), part)
    column_output = gaussian(seeds[5], (H * DH, C), (H * DH) ** -0.5, 0.375)
    transition_in = gaussian(seeds[6], (C, 2, FF), C ** -0.5, 0.375)
    transition_out = gaussian(seeds[7], (FF, C), FF ** -0.5, 0.1875)
    cotangent = bell_draw_with(part_splits[8], (S, R, C), 1.0, 6.0, ((0, 16),), (0, 1, 16, 2.0))
    return dict(alignment=alignment, pair_bias=pair_bias, row_project=row_project, row_output=row_output, column_project=column_project, column_output=column_output, transition_in=transition_in, transition_out=transition_out, cotangent=cotangent)


EPSILON = 1e-05

def product(pattern, former, latter):
    return jnp.einsum(pattern, former.astype(jnp.float32), latter.astype(jnp.float32))

def normalize(values):
    values = values.astype(jnp.float32)
    centred = values - lax.optimization_barrier(jnp.mean(values, axis=-1, keepdims=True))
    factor = lax.rsqrt(lax.optimization_barrier(jnp.mean(centred * centred, axis=-1, keepdims=True)) + EPSILON)
    return (centred * factor, factor)

def norm_back(normed, factor, upstream):
    mean_up = lax.optimization_barrier(jnp.mean(upstream, axis=-1, keepdims=True))
    mean_cross = lax.optimization_barrier(jnp.mean(upstream * normed, axis=-1, keepdims=True))
    return factor * (upstream - mean_up - normed * mean_cross)

def run_items(function, arrays, sequential):
    if sequential:
        return lax.map(lambda bundle: function(*bundle), arrays)
    return jax.vmap(function)(*arrays)

def head_shares(queries, key_rows, bias_head):
    scores = product('qd,kd->qk', queries, key_rows)
    if bias_head is not None:
        scores = scores + bias_head.astype(jnp.float32)
    row_top = lax.optimization_barrier(jnp.max(scores, axis=-1, keepdims=True))
    powered = jnp.exp(scores - row_top)
    return powered / lax.optimization_barrier(jnp.sum(powered, axis=-1, keepdims=True))

def head_forward(queries, key_rows, values, bias_head=None):
    shares = head_shares(queries, key_rows, bias_head)
    return product('qk,kd->qd', shares.astype(jnp.bfloat16), values)

def head_backward(queries, key_rows, values, grad_blend, bias_head=None):
    shares = head_shares(queries, key_rows, bias_head)
    shares_low = shares.astype(jnp.bfloat16)
    blended = product('qk,kd->qd', shares_low, values)
    grad_shares = product('qd,kd->qk', grad_blend, values)
    grad_values = product('qk,qd->kd', shares_low, grad_blend)
    centre = lax.optimization_barrier(jnp.sum(shares * grad_shares, axis=-1, keepdims=True))
    grad_scores = shares * (grad_shares - centre)
    grad_low = grad_scores.astype(jnp.bfloat16)
    grad_queries = product('qk,kd->qd', grad_low, key_rows)
    grad_keys = product('qk,qd->kd', grad_low, queries)
    return (blended, grad_queries, grad_keys, grad_values, grad_scores)

def item_project(normed_item, weights):
    projected = product('lc,cfhd->fhld', normed_item, weights.reshape(C, 4, H, DH))
    queries = (projected[0] * DH ** (-0.5)).astype(jnp.bfloat16)
    key_rows = projected[1].astype(jnp.bfloat16)
    values = projected[2].astype(jnp.bfloat16)
    gating = jax.nn.sigmoid(projected[3])
    return (queries, key_rows, values, gating)

def forward_item(normed_item, weights, bias_table, head_loop):
    queries, key_rows, values, gating = item_project(normed_item, weights)
    if bias_table is None:
        head_args = (queries, key_rows, values)
    else:
        head_args = (queries, key_rows, values, bias_table)
    blended = run_items(head_forward, head_args, head_loop)
    return (blended * gating).astype(jnp.bfloat16)

def backward_item(normed_item, upstream_item, weights, out_weight, bias_table, head_loop):
    queries, key_rows, values, gating = item_project(normed_item, weights)
    grad_gated = product('lc,hdc->hld', upstream_item, out_weight.reshape(H, DH, C))
    grad_blend = (grad_gated * gating).astype(jnp.bfloat16)
    if bias_table is None:
        head_args = (queries, key_rows, values, grad_blend)
    else:
        head_args = (queries, key_rows, values, grad_blend, bias_table)
    blended, grad_queries, grad_keys, grad_values, grad_scores = run_items(head_backward, head_args, head_loop)
    grad_gate = grad_gated * blended * gating * (1.0 - gating)
    grad_proj = jnp.stack([grad_queries * DH ** (-0.5), grad_keys, grad_values, grad_gate], axis=0).astype(jnp.bfloat16)
    if bias_table is None:
        return (grad_proj, jnp.zeros((), jnp.float32))
    return (grad_proj, grad_scores)

def section_forward(normed_low, weights, bias_table, item_loop, head_loop):

    def single(normed_item):
        return forward_item(normed_item, weights, bias_table, head_loop)
    return run_items(single, (normed_low,), item_loop)

def section_backward(normed_low, upstream_low, weights, out_weight, bias_table, item_loop, head_loop):

    def single(normed_item, upstream_item):
        return backward_item(normed_item, upstream_item, weights, out_weight, bias_table, head_loop)
    if bias_table is None:
        grad_proj, unused = run_items(single, (normed_low, upstream_low), item_loop)
        return (grad_proj, None)

    def accumulate(running, bundle):
        grad_proj, grad_scores = single(bundle[0], bundle[1])
        return (running + grad_scores, grad_proj)
    bias_total, grad_proj = lax.scan(accumulate, jnp.zeros(bias_table.shape, jnp.float32), (normed_low, upstream_low))
    return (grad_proj, bias_total)

def column_block(columns, upstream, column_project, column_output, transition_in, transition_out, item_loop, head_loop):
    normed_cols, scale_cols = normalize(columns)
    normed_cols_low = normed_cols.astype(jnp.bfloat16)
    column_gated = section_forward(normed_cols_low, column_project, None, item_loop, head_loop)
    column_update = product('bhld,hdc->blc', column_gated, column_output.reshape(H, DH, C))
    after_columns = (columns.astype(jnp.float32) + column_update).astype(jnp.bfloat16)
    normed_two, scale_two = normalize(after_columns)
    normed_two_low = normed_two.astype(jnp.bfloat16)
    pre_hidden = product('blc,cfe->blfe', normed_two_low, transition_in)
    gate_part = pre_hidden[:, :, 0]
    up_part = pre_hidden[:, :, 1]
    sigmoid_gate = jax.nn.sigmoid(gate_part)
    activated = gate_part * sigmoid_gate
    hidden = (activated * up_part).astype(jnp.bfloat16)
    raw_trans_out = product('blf,blc->fc', hidden, upstream)
    grad_hidden = product('blc,fc->blf', upstream, transition_out)
    grad_gate_part = grad_hidden * up_part * sigmoid_gate * (1.0 + gate_part * (1.0 - sigmoid_gate))
    grad_up_part = grad_hidden * activated
    grad_pre = jnp.stack([grad_gate_part, grad_up_part], axis=2).astype(jnp.bfloat16)
    raw_trans_in = product('blc,blfe->cfe', normed_two_low, grad_pre)
    grad_normed_two = product('blfe,cfe->blc', grad_pre, transition_in)
    grad_after_columns = upstream.astype(jnp.float32) + norm_back(normed_two, scale_two, grad_normed_two)
    grad_columns_low = grad_after_columns.astype(jnp.bfloat16)
    grad_proj, unused = section_backward(normed_cols_low, grad_columns_low, column_project, column_output, None, item_loop, head_loop)
    raw_column_output = product('bhld,blc->hdc', column_gated, grad_columns_low).reshape(H * DH, C)
    raw_column_project = product('blc,bfhld->cfhd', normed_cols_low, grad_proj).reshape(C, 4, H * DH)
    grad_normed_cols = product('bfhld,cfhd->blc', grad_proj, column_project.reshape(C, 4, H, DH))
    grad_after_rows = (grad_after_columns + norm_back(normed_cols, scale_cols, grad_normed_cols)).astype(jnp.bfloat16)
    return (grad_after_rows, raw_column_project, raw_column_output, raw_trans_in, raw_trans_out)

def row_block(normed_rows, scale_rows, normed_rows_low, row_gated, grad_after_rows, row_project, row_output, bias_table, head_loop):
    grad_proj, bias_total = section_backward(normed_rows_low, grad_after_rows, row_project, row_output, bias_table, True, head_loop)
    raw_row_output = product('bhld,blc->hdc', row_gated, grad_after_rows).reshape(H * DH, C)
    raw_row_project = product('blc,bfhld->cfhd', normed_rows_low, grad_proj).reshape(C, 4, H * DH)
    grad_normed_rows = product('bfhld,cfhd->blc', grad_proj, row_project.reshape(C, 4, H, DH))
    grad_alignment = (grad_after_rows.astype(jnp.float32) + norm_back(normed_rows, scale_rows, grad_normed_rows)).astype(jnp.bfloat16)
    return (grad_alignment, raw_row_project, raw_row_output, bias_total)

def reference(alignment, pair_bias, row_project, row_output, column_project, column_output, transition_in, transition_out, cotangent):
    normed_rows, scale_rows = normalize(alignment)
    normed_rows_low = normed_rows.astype(jnp.bfloat16)
    row_gated = section_forward(normed_rows_low, row_project, pair_bias, True, False)
    row_update = product('bhld,hdc->blc', row_gated, row_output.reshape(H, DH, C))
    after_rows = (alignment.astype(jnp.float32) + row_update).astype(jnp.bfloat16)
    columns = jnp.swapaxes(after_rows, 0, 1)
    upstream = jnp.swapaxes(cotangent, 0, 1)
    grad_columns, raw_column_project, raw_column_output, raw_trans_in, raw_trans_out = column_block(columns, upstream, column_project, column_output, transition_in, transition_out, True, False)
    grad_after_rows = jnp.swapaxes(grad_columns, 0, 1)
    grad_alignment, raw_row_project, raw_row_output, bias_total = row_block(normed_rows, scale_rows, normed_rows_low, row_gated, grad_after_rows, row_project, row_output, pair_bias, False)
    token_scale = (S * R) ** (-0.5)
    grad_bias = bias_total * (R * S ** (-0.5))
    return (grad_alignment, grad_bias, raw_row_project * token_scale, raw_row_output * token_scale, raw_column_project * token_scale, raw_column_output * token_scale, raw_trans_in * token_scale, raw_trans_out * token_scale)
```

```python
import jax
import jax.numpy as jnp
from jax import lax
from jax.experimental import pallas as pl
from jax.experimental.pallas import tpu as pltpu
from jax.sharding import PartitionSpec as P
import functools

C = 256
H = 8
DH = 32


EPSILON = 1e-05


def product(pattern, former, latter):
    return jnp.einsum(pattern, former, latter, preferred_element_type=jnp.float32)


def normalize(values):
    values = values.astype(jnp.float32)
    centred = values - jnp.mean(values, axis=-1, keepdims=True)
    factor = lax.rsqrt(jnp.mean(centred * centred, axis=-1, keepdims=True) + EPSILON)
    return (centred * factor, factor)


def norm_back(normed, factor, upstream):
    mean_up = jnp.mean(upstream, axis=-1, keepdims=True)
    mean_cross = jnp.mean(upstream * normed, axis=-1, keepdims=True)
    return factor * (upstream - mean_up - normed * mean_cross)


def run_items(function, arrays, sequential):
    if sequential:
        return lax.map(lambda bundle: function(*bundle), arrays)
    return jax.vmap(function)(*arrays)


def head_shares(queries, key_rows, bias_head):
    scores = product("qd,kd->qk", queries, key_rows)
    if bias_head is not None:
        scores = scores + bias_head.astype(jnp.float32)
    row_top = jnp.max(scores, axis=-1, keepdims=True)
    powered = jnp.exp(scores - row_top)
    return powered / jnp.sum(powered, axis=-1, keepdims=True)


def head_forward(queries, key_rows, values, bias_head=None):
    shares = head_shares(queries, key_rows, bias_head)
    return product("qk,kd->qd", shares.astype(jnp.bfloat16), values)


def head_backward(queries, key_rows, values, grad_blend, bias_head=None):
    shares = head_shares(queries, key_rows, bias_head)
    shares_low = shares.astype(jnp.bfloat16)
    blended = product("qk,kd->qd", shares_low, values)
    grad_shares = product("qd,kd->qk", grad_blend, values)
    grad_values = product("qk,qd->kd", shares_low, grad_blend)
    centre = jnp.sum(shares * grad_shares, axis=-1, keepdims=True)
    grad_scores = shares * (grad_shares - centre)
    grad_low = grad_scores.astype(jnp.bfloat16)
    grad_queries = product("qk,kd->qd", grad_low, key_rows)
    grad_keys = product("qk,qd->kd", grad_low, queries)
    return (blended, grad_queries, grad_keys, grad_values, grad_scores)


def item_project(normed_item, weights):
    projected = product("lc,cfhd->fhld", normed_item, weights.reshape(C, 4, H, DH))
    queries = (projected[0] * DH ** (-0.5)).astype(jnp.bfloat16)
    key_rows = projected[1].astype(jnp.bfloat16)
    values = projected[2].astype(jnp.bfloat16)
    gating = jax.nn.sigmoid(projected[3])
    return (queries, key_rows, values, gating)


def forward_item(normed_item, weights, bias_table, head_loop):
    queries, key_rows, values, gating = item_project(normed_item, weights)
    if bias_table is None:
        head_args = (queries, key_rows, values)
    else:
        head_args = (queries, key_rows, values, bias_table)
    blended = run_items(head_forward, head_args, head_loop)
    return (blended * gating).astype(jnp.bfloat16)


def backward_item(normed_item, upstream_item, weights, out_weight, bias_table, head_loop):
    queries, key_rows, values, gating = item_project(normed_item, weights)
    grad_gated = product("lc,hdc->hld", upstream_item, out_weight.reshape(H, DH, C))
    grad_blend = (grad_gated * gating).astype(jnp.bfloat16)
    if bias_table is None:
        head_args = (queries, key_rows, values, grad_blend)
    else:
        head_args = (queries, key_rows, values, grad_blend, bias_table)
    blended, grad_queries, grad_keys, grad_values, grad_scores = run_items(
        head_backward, head_args, head_loop
    )
    grad_gate = grad_gated * blended * gating * (1.0 - gating)
    grad_proj = jnp.stack(
        [grad_queries * DH ** (-0.5), grad_keys, grad_values, grad_gate], axis=0
    ).astype(jnp.bfloat16)
    if bias_table is None:
        return (grad_proj, jnp.zeros((), jnp.float32))
    return (grad_proj, grad_scores)


def section_forward(normed_low, weights, bias_table, item_loop, head_loop):

    def single(normed_item):
        return forward_item(normed_item, weights, bias_table, head_loop)

    return run_items(single, (normed_low,), item_loop)


def section_backward(
    normed_low, upstream_low, weights, out_weight, bias_table, item_loop, head_loop
):

    def single(normed_item, upstream_item):
        return backward_item(normed_item, upstream_item, weights, out_weight, bias_table, head_loop)

    if bias_table is None:
        grad_proj, unused = run_items(single, (normed_low, upstream_low), item_loop)
        return (grad_proj, None)

    def accumulate(running, bundle):
        grad_proj, grad_scores = single(bundle[0], bundle[1])
        return (running + grad_scores, grad_proj)

    bias_total, grad_proj = lax.scan(
        accumulate, jnp.zeros(bias_table.shape, jnp.float32), (normed_low, upstream_low)
    )
    return (grad_proj, bias_total)


def column_block(columns, upstream, column_project, column_output, transition_in, transition_out):
    normed_cols, scale_cols = normalize(columns)
    normed_cols_low = normed_cols.astype(jnp.bfloat16)
    column_gated = section_forward(normed_cols_low, column_project, None, False, False)
    column_update = product("bhld,hdc->blc", column_gated, column_output.reshape(H, DH, C))
    after_columns = (columns.astype(jnp.float32) + column_update).astype(jnp.bfloat16)
    normed_two, scale_two = normalize(after_columns)
    normed_two_low = normed_two.astype(jnp.bfloat16)
    pre_hidden = product("blc,cfe->blfe", normed_two_low, transition_in)
    gate_part = pre_hidden[:, :, 0]
    up_part = pre_hidden[:, :, 1]
    sigmoid_gate = jax.nn.sigmoid(gate_part)
    activated = gate_part * sigmoid_gate
    hidden = (activated * up_part).astype(jnp.bfloat16)
    raw_trans_out = product("blf,blc->fc", hidden, upstream)
    grad_hidden = product("blc,fc->blf", upstream, transition_out)
    grad_gate_part = grad_hidden * up_part * sigmoid_gate * (1.0 + gate_part * (1.0 - sigmoid_gate))
    grad_up_part = grad_hidden * activated
    grad_pre = jnp.stack([grad_gate_part, grad_up_part], axis=2).astype(jnp.bfloat16)
    raw_trans_in = product("blc,blfe->cfe", normed_two_low, grad_pre)
    grad_normed_two = product("blfe,cfe->blc", grad_pre, transition_in)
    grad_after_columns = upstream.astype(jnp.float32) + norm_back(
        normed_two, scale_two, grad_normed_two
    )
    grad_columns_low = grad_after_columns.astype(jnp.bfloat16)
    grad_proj, unused = section_backward(
        normed_cols_low, grad_columns_low, column_project, column_output, None, False, False
    )
    raw_column_output = product("bhld,blc->hdc", column_gated, grad_columns_low).reshape(H * DH, C)
    raw_column_project = product("blc,bfhld->cfhd", normed_cols_low, grad_proj).reshape(
        C, 4, H * DH
    )
    grad_normed_cols = product("bfhld,cfhd->blc", grad_proj, column_project.reshape(C, 4, H, DH))
    grad_after_rows = (
        grad_after_columns + norm_back(normed_cols, scale_cols, grad_normed_cols)
    ).astype(jnp.bfloat16)
    return (grad_after_rows, raw_column_project, raw_column_output, raw_trans_in, raw_trans_out)


def row_block(
    normed_rows,
    scale_rows,
    normed_rows_low,
    row_gated,
    grad_after_rows,
    row_project,
    row_output,
    bias_table,
):
    grad_proj, bias_total = section_backward(
        normed_rows_low, grad_after_rows, row_project, row_output, bias_table, True, True
    )
    raw_row_output = product("bhld,blc->hdc", row_gated, grad_after_rows).reshape(H * DH, C)
    raw_row_project = product("blc,bfhld->cfhd", normed_rows_low, grad_proj).reshape(C, 4, H * DH)
    grad_normed_rows = product("bfhld,cfhd->blc", grad_proj, row_project.reshape(C, 4, H, DH))
    grad_alignment = (
        grad_after_rows.astype(jnp.float32) + norm_back(normed_rows, scale_rows, grad_normed_rows)
    ).astype(jnp.bfloat16)
    return (grad_alignment, raw_row_project, raw_row_output, bias_total)


def to_columns(arranged):
    moved = lax.all_to_all(arranged, ("dap", "sub"), split_axis=1, concat_axis=0, tiled=True)
    return moved


def to_rows(arranged):
    moved = lax.all_to_all(arranged, ("dap", "sub"), split_axis=0, concat_axis=1, tiled=True)
    return moved


def split_shards(
    alignment,
    pair_bias,
    row_project,
    row_output,
    column_project,
    column_output,
    transition_in,
    transition_out,
    cotangent,
):
    bias_full = lax.all_gather(pair_bias, ("dap", "sub"), axis=1, tiled=True)
    upstream = jnp.swapaxes(to_columns(cotangent), 0, 1)
    normed_rows, scale_rows = normalize(alignment)
    normed_rows_low = normed_rows.astype(jnp.bfloat16)
    row_gated = section_forward(normed_rows_low, row_project, bias_full, True, True)
    row_update = product("bhld,hdc->blc", row_gated, row_output.reshape(H, DH, C))
    after_rows = (alignment.astype(jnp.float32) + row_update).astype(jnp.bfloat16)
    columns = jnp.swapaxes(to_columns(after_rows), 0, 1)
    grad_columns, raw_column_project, raw_column_output, raw_trans_in, raw_trans_out = column_block(
        columns, upstream, column_project, column_output, transition_in, transition_out
    )
    sequences = alignment.shape[0] * lax.axis_size("dap") * lax.axis_size("sub")
    residues = alignment.shape[1]
    token_scale = (sequences * residues) ** (-0.5)
    term_col_project = raw_column_project * token_scale
    term_col_output = raw_column_output * token_scale
    term_trans_in = raw_trans_in * token_scale
    term_trans_out = raw_trans_out * token_scale
    grad_after_rows = to_rows(jnp.swapaxes(grad_columns, 0, 1))
    grad_alignment, raw_row_project, raw_row_output, bias_total = row_block(
        normed_rows,
        scale_rows,
        normed_rows_low,
        row_gated,
        grad_after_rows,
        row_project,
        row_output,
        bias_full,
    )
    term_row_project = raw_row_project * token_scale
    term_row_output = raw_row_output * token_scale
    bias_term = bias_total * (residues * sequences ** (-0.5))
    grad_bias = lax.psum_scatter(bias_term, ("dap", "sub"), scatter_dimension=1, tiled=True)
    (
        grad_row_project,
        grad_row_output,
        grad_col_project,
        grad_col_output,
        grad_trans_in,
        grad_trans_out,
    ) = (
        lax.psum_scatter(term_row_project, ("dap", "sub"), scatter_dimension=0, tiled=True),
        lax.psum_scatter(term_row_output, ("dap", "sub"), scatter_dimension=0, tiled=True),
        lax.psum_scatter(term_col_project, ("dap", "sub"), scatter_dimension=0, tiled=True),
        lax.psum_scatter(term_col_output, ("dap", "sub"), scatter_dimension=0, tiled=True),
        lax.psum_scatter(term_trans_in, ("dap", "sub"), scatter_dimension=0, tiled=True),
        lax.psum_scatter(term_trans_out, ("dap", "sub"), scatter_dimension=0, tiled=True),
    )
    return (
        grad_alignment,
        grad_bias,
        grad_row_project,
        grad_row_output,
        grad_col_project,
        grad_col_output,
        grad_trans_in,
        grad_trans_out,
    )


LANES = 128
ROWS = 16
BF = jnp.bfloat16
F32 = jnp.float32
MESH = pl.DeviceIdType.MESH


def dot(a, b, left=1, right=0, precision=None):
    return lax.dot_general(
        a, b, (((left,), (right,)), ((), ())), preferred_element_type=F32, precision=precision
    )


def iota(shape, axis):
    return lax.broadcasted_iota(jnp.int32, shape, axis)


def one_hot(condition):
    return jnp.where(condition, 1.0, 0.0).astype(BF)


def own_rows(me, rows, total):
    return one_hot(iota((rows, total), 1) == me * rows + iota((rows, total), 0))


def gather_body(n, sub, x_ref, ct_ref, bias_ref, out_ref, send_sem, recv_sem):
    me = lax.axis_index("dap") * sub + lax.axis_index("sub")
    peers = [lax.rem(me + off, n) for off in range(1, n)]
    places = [{"dap": lax.div(p, sub), "sub": lax.rem(p, sub)} for p in peers]
    barrier = pltpu.get_barrier_semaphore()
    for place in places:
        pl.semaphore_signal(barrier, inc=1, device_id=place, device_id_type=MESH)
    residues = x_ref.shape[0]
    channels = x_ref.shape[1]
    heads, keys = bias_ref.shape
    mine = out_ref.at[me]
    mine[0:residues, :] = x_ref[...]
    mine[residues : 2 * residues, :] = ct_ref[...]
    spread = one_hot(lax.rem(iota((keys, channels), 1), keys) == iota((keys, channels), 0))
    tiled = dot(bias_ref[...], spread)
    padded = jnp.concatenate([tiled, jnp.zeros((ROWS - heads, channels), F32)], axis=0)
    mine[2 * residues : 2 * residues + ROWS, :] = padded.astype(BF)
    pl.semaphore_wait(barrier, n - 1)
    copies = []
    for off, place in enumerate(places):
        copies.append(
            pltpu.make_async_remote_copy(
                src_ref=mine,
                dst_ref=mine,
                send_sem=send_sem.at[off],
                recv_sem=recv_sem.at[off],
                device_id=place,
                device_id_type=MESH,
            )
        )
        copies[-1].start()
    for copy in copies:
        copy.wait()


def head_mask(h, width):
    return one_hot(lax.div(iota((1, width), 1), DH) == h)


def stack_heads(rows):
    width = rows.shape[1]
    return jnp.concatenate([rows * head_mask(h, width) for h in range(H)], axis=0)


def merge_heads(stacked):
    width = stacked.shape[1]
    group = stacked.shape[0] // H
    lane_head = lax.div(iota((1, width), 1), DH)
    total = stacked[0:group]
    for h in range(1, H):
        total = jnp.where(lane_head == h, stacked[h * group : (h + 1) * group], total)
    return total


def block_mask(group, length):
    shape = (H * group, group)
    query = lax.rem(iota(shape, 0), group)
    return jnp.where(lax.div(query, length) == lax.div(iota(shape, 1), length), 0.0, -1e30)


def project(low, weight_ref):
    parts = [dot(low, weight_ref[f]) for f in range(4)]
    queries = (parts[0] * DH ** (-0.5)).astype(BF)
    return queries, parts[1].astype(BF), parts[2].astype(BF), jax.nn.sigmoid(parts[3])


def attend(queries, keys, values, extra, group, shares_ref):
    blended = []
    for g in range(queries.shape[0] // group):
        rows = slice(g * group, (g + 1) * group)
        scores = dot(stack_heads(queries[rows]), keys[rows], 1, 1) + extra
        powered = jnp.exp(scores - jnp.max(scores, axis=-1, keepdims=True))
        shares = powered / jnp.sum(powered, axis=-1, keepdims=True)
        shares_ref[g] = shares
        blended.append(merge_heads(dot(shares.astype(BF), values[rows])))
    return jnp.concatenate(blended, axis=0)


def attend_back(queries, keys, values, gating, blended, upstream, out_weight, group, shares_ref, score_sink):
    grad_gated = dot(upstream, out_weight, 1, 1)
    grad_blend = (grad_gated * gating).astype(BF)
    grads = ([], [], [])
    for g in range(queries.shape[0] // group):
        rows = slice(g * group, (g + 1) * group)
        shares = shares_ref[g]
        blend_stack = stack_heads(grad_blend[rows])
        grad_shares = dot(blend_stack, values[rows], 1, 1)
        centre = jnp.sum(shares * grad_shares, axis=-1, keepdims=True)
        grad_scores = shares * (grad_shares - centre)
        grad_low = grad_scores.astype(BF)
        if score_sink is not None:
            score_sink(grad_scores, grad_low)
        grads[0].append(merge_heads(dot(grad_low, keys[rows])) * DH ** (-0.5))
        grads[1].append(dot(grad_low, stack_heads(queries[rows]), 0, 0))
        grads[2].append(dot(shares.astype(BF), blend_stack, 0, 0))
    grad_gate = grad_gated * blended * gating * (1.0 - gating)
    parts = [jnp.concatenate(part, axis=0) for part in grads] + [grad_gate]
    return [part.astype(BF) for part in parts]


def sample_body(
    n,
    sub,
    seqs,
    residues,
    all_ref,
    rp_in,
    ro_ref,
    cp_in,
    co_ref,
    ti_in,
    to_ref,
    g_x,
    g_bias,
    g_rp,
    g_ro,
    g_cp,
    g_co,
    g_ti,
    g_to,
    rp_ref,
    cp_ref,
    ti_ref,
    row_shares,
    col_shares,
):
    me = lax.axis_index("dap") * sub + lax.axis_index("sub")
    tokens = seqs * residues
    group = LANES
    scale = tokens ** (-0.5)
    for f in range(4):
        rp_ref[f] = rp_in[:, f, :]
        cp_ref[f] = cp_in[:, f, :]
    for f in range(2):
        ti_ref[f] = ti_in[:, f, :]

    x = all_ref[:, 0:residues, :].reshape(tokens, C)
    ct = all_ref[:, residues : 2 * residues, :].reshape(tokens, C)
    bias_rows = all_ref[:, 2 * residues : 2 * residues + ROWS, 0:LANES].reshape(n * ROWS, LANES)

    shape = (H * group, n * ROWS)
    row_at, col_at = iota(shape, 0), iota(shape, 1)
    pick = one_hot(
        (lax.div(col_at, ROWS) == lax.rem(row_at, residues))
        & (lax.rem(col_at, ROWS) == lax.div(row_at, group))
    )
    row_extra = dot(pick, bias_rows) + block_mask(group, residues)
    col_extra = block_mask(group, seqs)

    rows_f, scale_rows = normalize(x)
    rows_low = rows_f.astype(BF)
    rq, rk, rv, rgate = project(rows_low, rp_ref)
    rblend = attend(rq, rk, rv, row_extra, group, row_shares)
    row_gated = (rblend * rgate).astype(BF)
    after_rows = (x.astype(F32) + dot(row_gated, ro_ref[...])).astype(BF)

    square = (tokens, tokens)
    to_cols = one_hot(
        iota(square, 1) == lax.rem(iota(square, 0), seqs) * residues + lax.div(iota(square, 0), seqs)
    )
    columns = dot(to_cols, after_rows).astype(BF)
    upstream = dot(to_cols, ct).astype(BF)

    cols_f, scale_cols = normalize(columns)
    cols_low = cols_f.astype(BF)
    cq, ck, cv, cgate = project(cols_low, cp_ref)
    cblend = attend(cq, ck, cv, col_extra, group, col_shares)
    col_gated = (cblend * cgate).astype(BF)
    after_cols = (columns.astype(F32) + dot(col_gated, co_ref[...])).astype(BF)

    two_f, scale_two = normalize(after_cols)
    two_low = two_f.astype(BF)
    own_c = own_rows(me, C // n, C)
    two_own = dot(own_c, two_low, 1, 1).astype(BF)
    hidden_units = to_ref.shape[0]
    own_f = hidden_units // n
    chunk = C
    grad_two = None
    hidden_own = None
    for at in range(0, hidden_units, chunk):
        piece = slice(at, at + chunk)
        gate_part = dot(two_low, ti_ref[0, :, piece])
        up_part = dot(two_low, ti_ref[1, :, piece])
        sigmoid_gate = jax.nn.sigmoid(gate_part)
        activated = gate_part * sigmoid_gate
        hidden = (activated * up_part).astype(BF)
        select = one_hot(iota((own_f, chunk), 1) + at == me * own_f + iota((own_f, chunk), 0))
        held = dot(select, hidden, 1, 1)
        hidden_own = held if hidden_own is None else hidden_own + held
        grad_hidden = dot(upstream, to_ref[piece, :], 1, 1)
        grad_gate_part = (
            grad_hidden * up_part * sigmoid_gate * (1.0 + gate_part * (1.0 - sigmoid_gate))
        ).astype(BF)
        grad_up_part = (grad_hidden * activated).astype(BF)
        g_ti[:, 0, piece] = dot(two_own, grad_gate_part) * scale
        g_ti[:, 1, piece] = dot(two_own, grad_up_part) * scale
        part = dot(grad_gate_part, ti_ref[0, :, piece], 1, 1) + dot(
            grad_up_part, ti_ref[1, :, piece], 1, 1
        )
        grad_two = part if grad_two is None else grad_two + part
    g_to[...] = dot(hidden_own.astype(BF), upstream) * scale
    grad_after_cols = upstream.astype(F32) + norm_back(two_f, scale_two, grad_two)
    grad_cols_low = grad_after_cols.astype(BF)

    col_grads = attend_back(
        cq, ck, cv, cgate, cblend, grad_cols_low, co_ref[...], group, col_shares, None
    )
    g_co[...] = dot(dot(own_c, col_gated, 1, 1).astype(BF), grad_cols_low) * scale
    cols_own = dot(own_c, cols_low, 1, 1).astype(BF)
    grad_cols = None
    for f in range(4):
        g_cp[:, f, :] = dot(cols_own, col_grads[f]) * scale
        part = dot(col_grads[f], cp_ref[f], 1, 1)
        grad_cols = part if grad_cols is None else grad_cols + part
    grad_rows_cols = (grad_after_cols + norm_back(cols_f, scale_cols, grad_cols)).astype(BF)

    to_rows_hot = one_hot(
        iota(square, 1)
        == lax.rem(iota(square, 0), residues) * seqs + lax.div(iota(square, 0), residues)
    )
    grad_rows = dot(to_rows_hot, grad_rows_cols).astype(BF)

    bias_shape = (H, H * group)
    at_head, at_row = iota(bias_shape, 0), iota(bias_shape, 1)
    bias_pick = one_hot(
        (lax.div(at_row, group) == at_head) & (lax.rem(at_row, residues) == me)
    )
    bias_sums = []

    def sink(grad_scores, grad_low):
        rest = (grad_scores - grad_low.astype(F32)).astype(BF)
        bias_sums.append(dot(bias_pick, grad_low) + dot(bias_pick, rest))

    row_grads = attend_back(
        rq, rk, rv, rgate, rblend, grad_rows, ro_ref[...], group, row_shares, sink
    )
    bias_sum = bias_sums[0]
    for more in bias_sums[1:]:
        bias_sum = bias_sum + more
    folded = bias_sum[:, 0:residues]
    for at in range(residues, group, residues):
        folded = folded + bias_sum[:, at : at + residues]
    g_bias[:, 0, :] = folded * (residues * seqs ** (-0.5))

    g_ro[...] = dot(dot(own_c, row_gated, 1, 1).astype(BF), grad_rows) * scale
    rows_own = dot(own_c, rows_low, 1, 1).astype(BF)
    own_t = own_rows(me, residues, tokens)
    grad_own = None
    for f in range(4):
        g_rp[:, f, :] = dot(rows_own, row_grads[f]) * scale
        part = dot(dot(own_t, row_grads[f]).astype(BF), rp_ref[f], 1, 1)
        grad_own = part if grad_own is None else grad_own + part
    x_own, scale_own = normalize(all_ref[me, 0:residues, :])
    g_x[...] = (dot(own_t, grad_rows) + norm_back(x_own, scale_own, grad_own)).astype(BF)


def whole_shards(
    alignment,
    pair_bias,
    row_project,
    row_output,
    column_project,
    column_output,
    transition_in,
    transition_out,
    cotangent,
):
    sub = lax.axis_size("sub")
    n = lax.axis_size("dap") * sub
    residues = alignment.shape[1]
    seqs = n
    tokens = seqs * residues
    vmem = pl.BlockSpec(memory_space=pltpu.VMEM)
    gathered = pl.pallas_call(
        functools.partial(gather_body, n, sub),
        out_shape=jax.ShapeDtypeStruct((n, 2 * residues + ROWS, C), BF),
        in_specs=[vmem] * 3,
        out_specs=vmem,
        scratch_shapes=[pltpu.SemaphoreType.DMA((n - 1,)), pltpu.SemaphoreType.DMA((n - 1,))],
        compiler_params=pltpu.CompilerParams(collective_id=0, has_side_effects=True),
        name="gather_sample",
    )(
        alignment.reshape(residues, C),
        cotangent.reshape(residues, C),
        pair_bias.reshape(H, residues),
    )
    hidden_units = transition_out.shape[0]
    outs = (
        jax.ShapeDtypeStruct((residues, C), BF),
        jax.ShapeDtypeStruct((H, 1, residues), F32),
        jax.ShapeDtypeStruct((C // n, 4, H * DH), F32),
        jax.ShapeDtypeStruct((H * DH // n, C), F32),
        jax.ShapeDtypeStruct((C // n, 4, H * DH), F32),
        jax.ShapeDtypeStruct((H * DH // n, C), F32),
        jax.ShapeDtypeStruct((C // n, 2, hidden_units), F32),
        jax.ShapeDtypeStruct((hidden_units // n, C), F32),
    )
    results = pl.pallas_call(
        functools.partial(sample_body, n, sub, seqs, residues),
        out_shape=outs,
        in_specs=[vmem] * 7,
        out_specs=(vmem,) * 8,
        scratch_shapes=[
            pltpu.VMEM((4, C, H * DH), BF),
            pltpu.VMEM((4, C, H * DH), BF),
            pltpu.VMEM((2, C, hidden_units), BF),
            pltpu.VMEM((tokens // LANES, H * LANES, LANES), F32),
            pltpu.VMEM((tokens // LANES, H * LANES, LANES), F32),
        ],
        compiler_params=pltpu.CompilerParams(vmem_limit_bytes=48 * 1024 * 1024),
        name="sample_backward",
    )(gathered, row_project, row_output, column_project, column_output, transition_in, transition_out)
    return (results[0].reshape(alignment.shape),) + tuple(results[1:])


def shards(alignment, pair_bias, *rest):
    n = lax.axis_size("dap") * lax.axis_size("sub")
    residues = alignment.shape[1]
    tokens = alignment.shape[0] * n * residues
    fits = (
        alignment.shape[0] == 1
        and pair_bias.shape[1] == 1
        and residues % ROWS == 0
        and LANES % residues == 0
        and LANES % n == 0
        and tokens % LANES == 0
        and tokens <= 4 * LANES
    )
    if fits:
        return whole_shards(alignment, pair_bias, *rest)
    return split_shards(alignment, pair_bias, *rest)


def solution(mesh):
    in_specs = (
        P(("grp", "dap", "sub"), None, None),
        P(None, ("grp", "dap", "sub"), None),
        P(),
        P(),
        P(),
        P(),
        P(),
        P(),
        P(("grp", "dap", "sub"), None, None),
    )
    out_specs = (
        P(("grp", "dap", "sub"), None, None),
        P(None, ("grp", "dap", "sub"), None),
        P(("grp", "dap", "sub"), None, None),
        P(("grp", "dap", "sub"), None),
        P(("grp", "dap", "sub"), None, None),
        P(("grp", "dap", "sub"), None),
        P(("grp", "dap", "sub"), None, None),
        P(("grp", "dap", "sub"), None),
    )
    return jax.shard_map(shards, mesh=mesh, in_specs=in_specs, out_specs=out_specs, check_vma=False)
```

```python
import jax
import jax.numpy as jnp
from jax import lax
from jax.experimental import pallas as pl
from jax.experimental.pallas import tpu as pltpu
from jax.sharding import PartitionSpec as P
import functools

C = 256
H = 8
DH = 32


EPSILON = 1e-05


def product(pattern, former, latter):
    return jnp.einsum(pattern, former, latter, preferred_element_type=jnp.float32)


def normalize(values):
    values = values.astype(jnp.float32)
    centred = values - jnp.mean(values, axis=-1, keepdims=True)
    factor = lax.rsqrt(jnp.mean(centred * centred, axis=-1, keepdims=True) + EPSILON)
    return (centred * factor, factor)


def norm_back(normed, factor, upstream):
    mean_up = jnp.mean(upstream, axis=-1, keepdims=True)
    mean_cross = jnp.mean(upstream * normed, axis=-1, keepdims=True)
    return factor * (upstream - mean_up - normed * mean_cross)


def run_items(function, arrays, sequential):
    if sequential:
        return lax.map(lambda bundle: function(*bundle), arrays)
    return jax.vmap(function)(*arrays)


def head_shares(queries, key_rows, bias_head):
    scores = product("qd,kd->qk", queries, key_rows)
    if bias_head is not None:
        scores = scores + bias_head.astype(jnp.float32)
    row_top = jnp.max(scores, axis=-1, keepdims=True)
    powered = jnp.exp(scores - row_top)
    return powered / jnp.sum(powered, axis=-1, keepdims=True)


def head_forward(queries, key_rows, values, bias_head=None):
    shares = head_shares(queries, key_rows, bias_head)
    return product("qk,kd->qd", shares.astype(jnp.bfloat16), values)


def head_backward(queries, key_rows, values, grad_blend, bias_head=None):
    shares = head_shares(queries, key_rows, bias_head)
    shares_low = shares.astype(jnp.bfloat16)
    blended = product("qk,kd->qd", shares_low, values)
    grad_shares = product("qd,kd->qk", grad_blend, values)
    grad_values = product("qk,qd->kd", shares_low, grad_blend)
    centre = jnp.sum(shares * grad_shares, axis=-1, keepdims=True)
    grad_scores = shares * (grad_shares - centre)
    grad_low = grad_scores.astype(jnp.bfloat16)
    grad_queries = product("qk,kd->qd", grad_low, key_rows)
    grad_keys = product("qk,qd->kd", grad_low, queries)
    return (blended, grad_queries, grad_keys, grad_values, grad_scores)


def item_project(normed_item, weights):
    projected = product("lc,cfhd->fhld", normed_item, weights.reshape(C, 4, H, DH))
    queries = (projected[0] * DH ** (-0.5)).astype(jnp.bfloat16)
    key_rows = projected[1].astype(jnp.bfloat16)
    values = projected[2].astype(jnp.bfloat16)
    gating = jax.nn.sigmoid(projected[3])
    return (queries, key_rows, values, gating)


def forward_item(normed_item, weights, bias_table, head_loop):
    queries, key_rows, values, gating = item_project(normed_item, weights)
    if bias_table is None:
        head_args = (queries, key_rows, values)
    else:
        head_args = (queries, key_rows, values, bias_table)
    blended = run_items(head_forward, head_args, head_loop)
    return (blended * gating).astype(jnp.bfloat16)


def backward_item(normed_item, upstream_item, weights, out_weight, bias_table, head_loop):
    queries, key_rows, values, gating = item_project(normed_item, weights)
    grad_gated = product("lc,hdc->hld", upstream_item, out_weight.reshape(H, DH, C))
    grad_blend = (grad_gated * gating).astype(jnp.bfloat16)
    if bias_table is None:
        head_args = (queries, key_rows, values, grad_blend)
    else:
        head_args = (queries, key_rows, values, grad_blend, bias_table)
    blended, grad_queries, grad_keys, grad_values, grad_scores = run_items(
        head_backward, head_args, head_loop
    )
    grad_gate = grad_gated * blended * gating * (1.0 - gating)
    grad_proj = jnp.stack(
        [grad_queries * DH ** (-0.5), grad_keys, grad_values, grad_gate], axis=0
    ).astype(jnp.bfloat16)
    if bias_table is None:
        return (grad_proj, jnp.zeros((), jnp.float32))
    return (grad_proj, grad_scores)


def section_forward(normed_low, weights, bias_table, item_loop, head_loop):

    def single(normed_item):
        return forward_item(normed_item, weights, bias_table, head_loop)

    return run_items(single, (normed_low,), item_loop)


def section_backward(
    normed_low, upstream_low, weights, out_weight, bias_table, item_loop, head_loop
):

    def single(normed_item, upstream_item):
        return backward_item(normed_item, upstream_item, weights, out_weight, bias_table, head_loop)

    if bias_table is None:
        grad_proj, unused = run_items(single, (normed_low, upstream_low), item_loop)
        return (grad_proj, None)

    def accumulate(running, bundle):
        grad_proj, grad_scores = single(bundle[0], bundle[1])
        return (running + grad_scores, grad_proj)

    bias_total, grad_proj = lax.scan(
        accumulate, jnp.zeros(bias_table.shape, jnp.float32), (normed_low, upstream_low)
    )
    return (grad_proj, bias_total)


def column_block(columns, upstream, column_project, column_output, transition_in, transition_out):
    normed_cols, scale_cols = normalize(columns)
    normed_cols_low = normed_cols.astype(jnp.bfloat16)
    column_gated = section_forward(normed_cols_low, column_project, None, False, False)
    column_update = product("bhld,hdc->blc", column_gated, column_output.reshape(H, DH, C))
    after_columns = (columns.astype(jnp.float32) + column_update).astype(jnp.bfloat16)
    normed_two, scale_two = normalize(after_columns)
    normed_two_low = normed_two.astype(jnp.bfloat16)
    pre_hidden = product("blc,cfe->blfe", normed_two_low, transition_in)
    gate_part = pre_hidden[:, :, 0]
    up_part = pre_hidden[:, :, 1]
    sigmoid_gate = jax.nn.sigmoid(gate_part)
    activated = gate_part * sigmoid_gate
    hidden = (activated * up_part).astype(jnp.bfloat16)
    raw_trans_out = product("blf,blc->fc", hidden, upstream)
    grad_hidden = product("blc,fc->blf", upstream, transition_out)
    grad_gate_part = grad_hidden * up_part * sigmoid_gate * (1.0 + gate_part * (1.0 - sigmoid_gate))
    grad_up_part = grad_hidden * activated
    grad_pre = jnp.stack([grad_gate_part, grad_up_part], axis=2).astype(jnp.bfloat16)
    raw_trans_in = product("blc,blfe->cfe", normed_two_low, grad_pre)
    grad_normed_two = product("blfe,cfe->blc", grad_pre, transition_in)
    grad_after_columns = upstream.astype(jnp.float32) + norm_back(
        normed_two, scale_two, grad_normed_two
    )
    grad_columns_low = grad_after_columns.astype(jnp.bfloat16)
    grad_proj, unused = section_backward(
        normed_cols_low, grad_columns_low, column_project, column_output, None, False, False
    )
    raw_column_output = product("bhld,blc->hdc", column_gated, grad_columns_low).reshape(H * DH, C)
    raw_column_project = product("blc,bfhld->cfhd", normed_cols_low, grad_proj).reshape(
        C, 4, H * DH
    )
    grad_normed_cols = product("bfhld,cfhd->blc", grad_proj, column_project.reshape(C, 4, H, DH))
    grad_after_rows = (
        grad_after_columns + norm_back(normed_cols, scale_cols, grad_normed_cols)
    ).astype(jnp.bfloat16)
    return (grad_after_rows, raw_column_project, raw_column_output, raw_trans_in, raw_trans_out)


def row_block(
    normed_rows,
    scale_rows,
    normed_rows_low,
    row_gated,
    grad_after_rows,
    row_project,
    row_output,
    bias_table,
):
    grad_proj, bias_total = section_backward(
        normed_rows_low, grad_after_rows, row_project, row_output, bias_table, True, True
    )
    raw_row_output = product("bhld,blc->hdc", row_gated, grad_after_rows).reshape(H * DH, C)
    raw_row_project = product("blc,bfhld->cfhd", normed_rows_low, grad_proj).reshape(C, 4, H * DH)
    grad_normed_rows = product("bfhld,cfhd->blc", grad_proj, row_project.reshape(C, 4, H, DH))
    grad_alignment = (
        grad_after_rows.astype(jnp.float32) + norm_back(normed_rows, scale_rows, grad_normed_rows)
    ).astype(jnp.bfloat16)
    return (grad_alignment, raw_row_project, raw_row_output, bias_total)


def to_columns(arranged):
    moved = lax.all_to_all(arranged, ("dap", "sub"), split_axis=1, concat_axis=0, tiled=True)
    return moved


def to_rows(arranged):
    moved = lax.all_to_all(arranged, ("dap", "sub"), split_axis=0, concat_axis=1, tiled=True)
    return moved


def split_shards(
    alignment,
    pair_bias,
    row_project,
    row_output,
    column_project,
    column_output,
    transition_in,
    transition_out,
    cotangent,
):
    bias_full = lax.all_gather(pair_bias, ("dap", "sub"), axis=1, tiled=True)
    upstream = jnp.swapaxes(to_columns(cotangent), 0, 1)
    normed_rows, scale_rows = normalize(alignment)
    normed_rows_low = normed_rows.astype(jnp.bfloat16)
    row_gated = section_forward(normed_rows_low, row_project, bias_full, True, True)
    row_update = product("bhld,hdc->blc", row_gated, row_output.reshape(H, DH, C))
    after_rows = (alignment.astype(jnp.float32) + row_update).astype(jnp.bfloat16)
    columns = jnp.swapaxes(to_columns(after_rows), 0, 1)
    grad_columns, raw_column_project, raw_column_output, raw_trans_in, raw_trans_out = column_block(
        columns, upstream, column_project, column_output, transition_in, transition_out
    )
    sequences = alignment.shape[0] * lax.axis_size("dap") * lax.axis_size("sub")
    residues = alignment.shape[1]
    token_scale = (sequences * residues) ** (-0.5)
    term_col_project = raw_column_project * token_scale
    term_col_output = raw_column_output * token_scale
    term_trans_in = raw_trans_in * token_scale
    term_trans_out = raw_trans_out * token_scale
    grad_after_rows = to_rows(jnp.swapaxes(grad_columns, 0, 1))
    grad_alignment, raw_row_project, raw_row_output, bias_total = row_block(
        normed_rows,
        scale_rows,
        normed_rows_low,
        row_gated,
        grad_after_rows,
        row_project,
        row_output,
        bias_full,
    )
    term_row_project = raw_row_project * token_scale
    term_row_output = raw_row_output * token_scale
    bias_term = bias_total * (residues * sequences ** (-0.5))
    grad_bias = lax.psum_scatter(bias_term, ("dap", "sub"), scatter_dimension=1, tiled=True)
    (
        grad_row_project,
        grad_row_output,
        grad_col_project,
        grad_col_output,
        grad_trans_in,
        grad_trans_out,
    ) = (
        lax.psum_scatter(term_row_project, ("dap", "sub"), scatter_dimension=0, tiled=True),
        lax.psum_scatter(term_row_output, ("dap", "sub"), scatter_dimension=0, tiled=True),
        lax.psum_scatter(term_col_project, ("dap", "sub"), scatter_dimension=0, tiled=True),
        lax.psum_scatter(term_col_output, ("dap", "sub"), scatter_dimension=0, tiled=True),
        lax.psum_scatter(term_trans_in, ("dap", "sub"), scatter_dimension=0, tiled=True),
        lax.psum_scatter(term_trans_out, ("dap", "sub"), scatter_dimension=0, tiled=True),
    )
    return (
        grad_alignment,
        grad_bias,
        grad_row_project,
        grad_row_output,
        grad_col_project,
        grad_col_output,
        grad_trans_in,
        grad_trans_out,
    )


LANES = 128
ROWS = 16
BF = jnp.bfloat16
F32 = jnp.float32
MESH = pl.DeviceIdType.MESH


def dot(a, b, left=1, right=0, precision=None):
    return lax.dot_general(
        a, b, (((left,), (right,)), ((), ())), preferred_element_type=F32, precision=precision
    )


def iota(shape, axis):
    return lax.broadcasted_iota(jnp.int32, shape, axis)


def one_hot(condition):
    return jnp.where(condition, 1.0, 0.0).astype(BF)


def own_rows(me, rows, total):
    return one_hot(iota((rows, total), 1) == me * rows + iota((rows, total), 0))


def gang(nd, nz, oz, od):
    d, z = lax.axis_index("dap"), lax.axis_index("sub")
    return lax.rem(d + od, nd), lax.rem(z + oz, nz)


def send(buffer, slot, d, z, send_sem, recv_sem):
    return pltpu.make_async_remote_copy(
        src_ref=buffer.at[slot],
        dst_ref=buffer.at[slot],
        send_sem=send_sem,
        recv_sem=recv_sem,
        device_id={"dap": d, "sub": z},
        device_id_type=MESH,
    )


def spread_own(nd, nz, buffer, send_sem, recv_sem):
    me = lax.axis_index("dap") * nz + lax.axis_index("sub")
    copies = {}
    for oz in range(1, nz):
        d, z = gang(nd, nz, oz, 0)
        copies[oz, 0] = send(buffer, me, d, z, send_sem.at[oz, 0], recv_sem.at[oz, 0])
        copies[oz, 0].start()
    for od in range(1, nd):
        d, z = gang(nd, nz, 0, od)
        copies[0, od] = send(buffer, me, d, z, send_sem.at[0, od], recv_sem.at[0, od])
        copies[0, od].start()
    return copies


def relay(nd, nz, buffer, send_sem, recv_sem, copies):
    for oz in range(1, nz):
        copies[oz, 0].wait_recv()
        from_d, from_z = gang(nd, nz, nz - oz, 0)
        slot = from_d * nz + from_z
        for od in range(1, nd):
            d, z = gang(nd, nz, 0, od)
            copies[oz, od] = send(buffer, slot, d, z, send_sem.at[oz, od], recv_sem.at[oz, od])
            copies[oz, od].start()


def collect(copies):
    for (oz, od), copy in copies.items():
        if od:
            copy.wait_recv()


def head_mask(h, width):
    return one_hot(lax.div(iota((1, width), 1), DH) == h)


def stack_heads(rows):
    width = rows.shape[1]
    return jnp.concatenate([rows * head_mask(h, width) for h in range(H)], axis=0)


def merge_heads(stacked):
    width = stacked.shape[1]
    group = stacked.shape[0] // H
    lane_head = lax.div(iota((1, width), 1), DH)
    total = stacked[0:group]
    for h in range(1, H):
        total = jnp.where(lane_head == h, stacked[h * group : (h + 1) * group], total)
    return total


def block_mask(group, length):
    shape = (H * group, group)
    query = lax.rem(iota(shape, 0), group)
    return jnp.where(lax.div(query, length) == lax.div(iota(shape, 1), length), 0.0, -1e30)


def project(low, weight_ref):
    parts = [dot(low, weight_ref[f]) for f in range(4)]
    queries = (parts[0] * DH ** (-0.5)).astype(BF)
    return queries, parts[1].astype(BF), parts[2].astype(BF), jax.nn.sigmoid(parts[3])


def attend(queries, keys, values, extra, group, shares_ref):
    blended = []
    for g in range(queries.shape[0] // group):
        rows = slice(g * group, (g + 1) * group)
        scores = dot(stack_heads(queries[rows]), keys[rows], 1, 1) + extra
        powered = jnp.exp(scores - jnp.max(scores, axis=-1, keepdims=True))
        shares = powered / jnp.sum(powered, axis=-1, keepdims=True)
        shares_ref[g] = shares
        blended.append(merge_heads(dot(shares.astype(BF), values[rows])))
    return jnp.concatenate(blended, axis=0)


def attend_back(queries, keys, values, gating, blended, upstream, out_weight, group, shares_ref, score_sink):
    grad_gated = dot(upstream, out_weight, 1, 1)
    grad_blend = (grad_gated * gating).astype(BF)
    grads = ([], [], [])
    for g in range(queries.shape[0] // group):
        rows = slice(g * group, (g + 1) * group)
        shares = shares_ref[g]
        blend_stack = stack_heads(grad_blend[rows])
        grad_shares = dot(blend_stack, values[rows], 1, 1)
        centre = jnp.sum(shares * grad_shares, axis=-1, keepdims=True)
        grad_scores = shares * (grad_shares - centre)
        grad_low = grad_scores.astype(BF)
        if score_sink is not None:
            score_sink(grad_scores, grad_low)
        grads[0].append(merge_heads(dot(grad_low, keys[rows])) * DH ** (-0.5))
        grads[1].append(dot(grad_low, stack_heads(queries[rows]), 0, 0))
        grads[2].append(dot(shares.astype(BF), blend_stack, 0, 0))
    grad_gate = grad_gated * blended * gating * (1.0 - gating)
    parts = [jnp.concatenate(part, axis=0) for part in grads] + [grad_gate]
    return [part.astype(BF) for part in parts]


def sample_body(
    nd,
    nz,
    x_in,
    ct_in,
    bias_in,
    rp_hbm,
    ro_hbm,
    cp_hbm,
    co_hbm,
    ti_hbm,
    to_hbm,
    g_x,
    g_bias,
    g_rp,
    g_ro,
    g_cp,
    g_co,
    g_ti,
    g_to,
    x_all,
    ct_all,
    rp_in,
    ro_ref,
    cp_in,
    co_ref,
    ti_in,
    to_ref,
    rp_ref,
    cp_ref,
    ti_ref,
    row_shares,
    col_shares,
    load_sem,
    x_send,
    x_recv,
    ct_send,
    ct_recv,
):
    n = nd * nz
    me = lax.axis_index("dap") * nz + lax.axis_index("sub")
    barrier = pltpu.get_barrier_semaphore()
    for oz in range(nz):
        for od in range(nd):
            if (oz == 0) != (od == 0):
                d, z = gang(nd, nz, oz, od)
                pl.semaphore_signal(
                    barrier, inc=1, device_id={"dap": d, "sub": z}, device_id_type=MESH
                )
    sources = (rp_hbm, cp_hbm, ti_hbm, ro_hbm, co_hbm, to_hbm)
    targets = (rp_in, cp_in, ti_in, ro_ref, co_ref, to_ref)
    loads = [
        pltpu.make_async_copy(source, target, load_sem.at[i])
        for i, (source, target) in enumerate(zip(sources, targets))
    ]
    for load in loads:
        load.start()
    residues = x_in.shape[0]
    seqs = n
    tokens = seqs * residues
    group = LANES
    scale = tokens ** (-0.5)
    spread = one_hot(lax.rem(iota((residues, LANES), 1), residues) == iota((residues, LANES), 0))
    tiled = dot(bias_in[...], spread)
    padded = jnp.concatenate([tiled, jnp.zeros((ROWS - H, LANES), F32)], axis=0).astype(BF)
    x_all[me, :, 0:C] = x_in[...]
    x_all[me, 0:ROWS, C : C + LANES] = padded
    ct_all[me] = ct_in[...]
    pl.semaphore_wait(barrier, nz + nd - 2)
    x_copies = spread_own(nd, nz, x_all, x_send, x_recv)
    ct_copies = spread_own(nd, nz, ct_all, ct_send, ct_recv)
    relay(nd, nz, x_all, x_send, x_recv, x_copies)
    loads[0].wait()
    for f in range(4):
        rp_ref[f] = rp_in[:, f, :]
    loads[1].wait()
    for f in range(4):
        cp_ref[f] = cp_in[:, f, :]
    relay(nd, nz, ct_all, ct_send, ct_recv, ct_copies)
    loads[2].wait()
    for f in range(2):
        ti_ref[f] = ti_in[:, f, :]
    for load in loads[3:]:
        load.wait()
    collect(x_copies)

    x = x_all[:, :, 0:C].reshape(tokens, C)
    bias_rows = x_all[:, 0:ROWS, C : C + LANES].reshape(n * ROWS, LANES)

    shape = (H * group, n * ROWS)
    row_at, col_at = iota(shape, 0), iota(shape, 1)
    pick = one_hot(
        (lax.div(col_at, ROWS) == lax.rem(row_at, residues))
        & (lax.rem(col_at, ROWS) == lax.div(row_at, group))
    )
    row_extra = dot(pick, bias_rows) + block_mask(group, residues)
    col_extra = block_mask(group, seqs)

    rows_f, scale_rows = normalize(x)
    rows_low = rows_f.astype(BF)
    rq, rk, rv, rgate = project(rows_low, rp_ref)
    rblend = attend(rq, rk, rv, row_extra, group, row_shares)
    row_gated = (rblend * rgate).astype(BF)
    after_rows = (x.astype(F32) + dot(row_gated, ro_ref[...])).astype(BF)

    square = (tokens, tokens)
    to_cols = one_hot(
        iota(square, 1) == lax.rem(iota(square, 0), seqs) * residues + lax.div(iota(square, 0), seqs)
    )
    columns = dot(to_cols, after_rows).astype(BF)

    cols_f, scale_cols = normalize(columns)
    cols_low = cols_f.astype(BF)
    cq, ck, cv, cgate = project(cols_low, cp_ref)
    cblend = attend(cq, ck, cv, col_extra, group, col_shares)
    col_gated = (cblend * cgate).astype(BF)
    after_cols = (columns.astype(F32) + dot(col_gated, co_ref[...])).astype(BF)

    collect(ct_copies)
    ct = ct_all[...].reshape(tokens, C)
    upstream = dot(to_cols, ct).astype(BF)

    two_f, scale_two = normalize(after_cols)
    two_low = two_f.astype(BF)
    own_c = own_rows(me, C // n, C)
    two_own = dot(own_c, two_low, 1, 1).astype(BF)
    hidden_units = to_ref.shape[0]
    own_f = hidden_units // n
    chunk = C
    grad_two = None
    hidden_own = None
    for at in range(0, hidden_units, chunk):
        piece = slice(at, at + chunk)
        gate_part = dot(two_low, ti_ref[0, :, piece])
        up_part = dot(two_low, ti_ref[1, :, piece])
        sigmoid_gate = jax.nn.sigmoid(gate_part)
        activated = gate_part * sigmoid_gate
        hidden = (activated * up_part).astype(BF)
        select = one_hot(iota((own_f, chunk), 1) + at == me * own_f + iota((own_f, chunk), 0))
        held = dot(select, hidden, 1, 1)
        hidden_own = held if hidden_own is None else hidden_own + held
        grad_hidden = dot(upstream, to_ref[piece, :], 1, 1)
        grad_gate_part = (
            grad_hidden * up_part * sigmoid_gate * (1.0 + gate_part * (1.0 - sigmoid_gate))
        ).astype(BF)
        grad_up_part = (grad_hidden * activated).astype(BF)
        g_ti[:, 0, piece] = dot(two_own, grad_gate_part) * scale
        g_ti[:, 1, piece] = dot(two_own, grad_up_part) * scale
        part = dot(grad_gate_part, ti_ref[0, :, piece], 1, 1) + dot(
            grad_up_part, ti_ref[1, :, piece], 1, 1
        )
        grad_two = part if grad_two is None else grad_two + part
    g_to[...] = dot(hidden_own.astype(BF), upstream) * scale
    grad_after_cols = upstream.astype(F32) + norm_back(two_f, scale_two, grad_two)
    grad_cols_low = grad_after_cols.astype(BF)

    col_grads = attend_back(
        cq, ck, cv, cgate, cblend, grad_cols_low, co_ref[...], group, col_shares, None
    )
    g_co[...] = dot(dot(own_c, col_gated, 1, 1).astype(BF), grad_cols_low) * scale
    cols_own = dot(own_c, cols_low, 1, 1).astype(BF)
    grad_cols = None
    for f in range(4):
        g_cp[:, f, :] = dot(cols_own, col_grads[f]) * scale
        part = dot(col_grads[f], cp_ref[f], 1, 1)
        grad_cols = part if grad_cols is None else grad_cols + part
    grad_rows_cols = (grad_after_cols + norm_back(cols_f, scale_cols, grad_cols)).astype(BF)

    to_rows_hot = one_hot(
        iota(square, 1)
        == lax.rem(iota(square, 0), residues) * seqs + lax.div(iota(square, 0), residues)
    )
    grad_rows = dot(to_rows_hot, grad_rows_cols).astype(BF)

    bias_shape = (H, H * group)
    at_head, at_row = iota(bias_shape, 0), iota(bias_shape, 1)
    bias_pick = one_hot(
        (lax.div(at_row, group) == at_head) & (lax.rem(at_row, residues) == me)
    )
    bias_sums = []

    def sink(grad_scores, grad_low):
        rest = (grad_scores - grad_low.astype(F32)).astype(BF)
        bias_sums.append(dot(bias_pick, grad_low) + dot(bias_pick, rest))

    row_grads = attend_back(
        rq, rk, rv, rgate, rblend, grad_rows, ro_ref[...], group, row_shares, sink
    )
    bias_sum = bias_sums[0]
    for more in bias_sums[1:]:
        bias_sum = bias_sum + more
    folded = bias_sum[:, 0:residues]
    for at in range(residues, group, residues):
        folded = folded + bias_sum[:, at : at + residues]
    g_bias[:, 0, :] = folded * (residues * seqs ** (-0.5))

    g_ro[...] = dot(dot(own_c, row_gated, 1, 1).astype(BF), grad_rows) * scale
    rows_own = dot(own_c, rows_low, 1, 1).astype(BF)
    own_t = own_rows(me, residues, tokens)
    grad_own = None
    for f in range(4):
        g_rp[:, f, :] = dot(rows_own, row_grads[f]) * scale
        part = dot(dot(own_t, row_grads[f]).astype(BF), rp_ref[f], 1, 1)
        grad_own = part if grad_own is None else grad_own + part
    x_own, scale_own = normalize(x_in[...])
    g_x[...] = (dot(own_t, grad_rows) + norm_back(x_own, scale_own, grad_own)).astype(BF)
    for copy in list(x_copies.values()) + list(ct_copies.values()):
        copy.wait_send()


def whole_shards(
    alignment,
    pair_bias,
    row_project,
    row_output,
    column_project,
    column_output,
    transition_in,
    transition_out,
    cotangent,
):
    nd, nz = lax.axis_size("dap"), lax.axis_size("sub")
    n = nd * nz
    residues = alignment.shape[1]
    tokens = n * residues
    vmem = pl.BlockSpec(memory_space=pltpu.VMEM)
    hbm = pl.BlockSpec(memory_space=pl.ANY)
    hidden_units = transition_out.shape[0]
    outs = (
        jax.ShapeDtypeStruct((residues, C), BF),
        jax.ShapeDtypeStruct((H, 1, residues), F32),
        jax.ShapeDtypeStruct((C // n, 4, H * DH), F32),
        jax.ShapeDtypeStruct((H * DH // n, C), F32),
        jax.ShapeDtypeStruct((C // n, 4, H * DH), F32),
        jax.ShapeDtypeStruct((H * DH // n, C), F32),
        jax.ShapeDtypeStruct((C // n, 2, hidden_units), F32),
        jax.ShapeDtypeStruct((hidden_units // n, C), F32),
    )
    weights = (
        row_project,
        row_output,
        column_project,
        column_output,
        transition_in,
        transition_out,
    )
    results = pl.pallas_call(
        functools.partial(sample_body, nd, nz),
        out_shape=outs,
        in_specs=[vmem] * 3 + [hbm] * 6,
        out_specs=(vmem,) * 8,
        scratch_shapes=[
            pltpu.VMEM((n, residues, C + LANES), BF),
            pltpu.VMEM((n, residues, C), BF),
        ]
        + [pltpu.VMEM(weight.shape, BF) for weight in weights]
        + [
            pltpu.VMEM((4, C, H * DH), BF),
            pltpu.VMEM((4, C, H * DH), BF),
            pltpu.VMEM((2, C, hidden_units), BF),
            pltpu.VMEM((tokens // LANES, H * LANES, LANES), F32),
            pltpu.VMEM((tokens // LANES, H * LANES, LANES), F32),
            pltpu.SemaphoreType.DMA((len(weights),)),
        ]
        + [pltpu.SemaphoreType.DMA((nz, nd))] * 4,
        compiler_params=pltpu.CompilerParams(
            collective_id=0, has_side_effects=True, vmem_limit_bytes=63 * 1024 * 1024
        ),
        name="sample_backward",
    )(
        alignment.reshape(residues, C),
        cotangent.reshape(residues, C),
        pair_bias.reshape(H, residues),
        *weights,
    )
    return (results[0].reshape(alignment.shape),) + tuple(results[1:])


def shards(alignment, pair_bias, *rest):
    n = lax.axis_size("dap") * lax.axis_size("sub")
    residues = alignment.shape[1]
    tokens = alignment.shape[0] * n * residues
    fits = (
        alignment.shape[0] == 1
        and pair_bias.shape[1] == 1
        and residues >= ROWS
        and residues % ROWS == 0
        and H <= ROWS
        and LANES % residues == 0
        and LANES % n == 0
        and tokens % LANES == 0
        and tokens <= 4 * LANES
    )
    if fits:
        return whole_shards(alignment, pair_bias, *rest)
    return split_shards(alignment, pair_bias, *rest)


def solution(mesh):
    in_specs = (
        P(("grp", "dap", "sub"), None, None),
        P(None, ("grp", "dap", "sub"), None),
        P(),
        P(),
        P(),
        P(),
        P(),
        P(),
        P(("grp", "dap", "sub"), None, None),
    )
    out_specs = (
        P(("grp", "dap", "sub"), None, None),
        P(None, ("grp", "dap", "sub"), None),
        P(("grp", "dap", "sub"), None, None),
        P(("grp", "dap", "sub"), None),
        P(("grp", "dap", "sub"), None, None),
        P(("grp", "dap", "sub"), None),
        P(("grp", "dap", "sub"), None, None),
        P(("grp", "dap", "sub"), None),
    )
    return jax.shard_map(shards, mesh=mesh, in_specs=in_specs, out_specs=out_specs, check_vma=False)
```

```python
import jax
import jax.numpy as jnp
from jax import lax
from jax.experimental import pallas as pl
from jax.experimental.pallas import tpu as pltpu
from jax.sharding import PartitionSpec as P
import functools

C = 256
H = 8
DH = 32


EPSILON = 1e-05


def product(pattern, former, latter):
    return jnp.einsum(pattern, former, latter, preferred_element_type=jnp.float32)


def normalize(values):
    values = values.astype(jnp.float32)
    centred = values - jnp.mean(values, axis=-1, keepdims=True)
    factor = lax.rsqrt(jnp.mean(centred * centred, axis=-1, keepdims=True) + EPSILON)
    return (centred * factor, factor)


def norm_back(normed, factor, upstream):
    mean_up = jnp.mean(upstream, axis=-1, keepdims=True)
    mean_cross = jnp.mean(upstream * normed, axis=-1, keepdims=True)
    return factor * (upstream - mean_up - normed * mean_cross)


def run_items(function, arrays, sequential):
    if sequential:
        return lax.map(lambda bundle: function(*bundle), arrays)
    return jax.vmap(function)(*arrays)


def head_shares(queries, key_rows, bias_head):
    scores = product("qd,kd->qk", queries, key_rows)
    if bias_head is not None:
        scores = scores + bias_head.astype(jnp.float32)
    row_top = jnp.max(scores, axis=-1, keepdims=True)
    powered = jnp.exp(scores - row_top)
    return powered / jnp.sum(powered, axis=-1, keepdims=True)


def head_forward(queries, key_rows, values, bias_head=None):
    shares = head_shares(queries, key_rows, bias_head)
    return product("qk,kd->qd", shares.astype(jnp.bfloat16), values)


def head_backward(queries, key_rows, values, grad_blend, bias_head=None):
    shares = head_shares(queries, key_rows, bias_head)
    shares_low = shares.astype(jnp.bfloat16)
    blended = product("qk,kd->qd", shares_low, values)
    grad_shares = product("qd,kd->qk", grad_blend, values)
    grad_values = product("qk,qd->kd", shares_low, grad_blend)
    centre = jnp.sum(shares * grad_shares, axis=-1, keepdims=True)
    grad_scores = shares * (grad_shares - centre)
    grad_low = grad_scores.astype(jnp.bfloat16)
    grad_queries = product("qk,kd->qd", grad_low, key_rows)
    grad_keys = product("qk,qd->kd", grad_low, queries)
    return (blended, grad_queries, grad_keys, grad_values, grad_scores)


def item_project(normed_item, weights):
    projected = product("lc,cfhd->fhld", normed_item, weights.reshape(C, 4, H, DH))
    queries = (projected[0] * DH ** (-0.5)).astype(jnp.bfloat16)
    key_rows = projected[1].astype(jnp.bfloat16)
    values = projected[2].astype(jnp.bfloat16)
    gating = jax.nn.sigmoid(projected[3])
    return (queries, key_rows, values, gating)


def forward_item(normed_item, weights, bias_table, head_loop):
    queries, key_rows, values, gating = item_project(normed_item, weights)
    if bias_table is None:
        head_args = (queries, key_rows, values)
    else:
        head_args = (queries, key_rows, values, bias_table)
    blended = run_items(head_forward, head_args, head_loop)
    return (blended * gating).astype(jnp.bfloat16)


def backward_item(normed_item, upstream_item, weights, out_weight, bias_table, head_loop):
    queries, key_rows, values, gating = item_project(normed_item, weights)
    grad_gated = product("lc,hdc->hld", upstream_item, out_weight.reshape(H, DH, C))
    grad_blend = (grad_gated * gating).astype(jnp.bfloat16)
    if bias_table is None:
        head_args = (queries, key_rows, values, grad_blend)
    else:
        head_args = (queries, key_rows, values, grad_blend, bias_table)
    blended, grad_queries, grad_keys, grad_values, grad_scores = run_items(
        head_backward, head_args, head_loop
    )
    grad_gate = grad_gated * blended * gating * (1.0 - gating)
    grad_proj = jnp.stack(
        [grad_queries * DH ** (-0.5), grad_keys, grad_values, grad_gate], axis=0
    ).astype(jnp.bfloat16)
    if bias_table is None:
        return (grad_proj, jnp.zeros((), jnp.float32))
    return (grad_proj, grad_scores)


def section_forward(normed_low, weights, bias_table, item_loop, head_loop):

    def single(normed_item):
        return forward_item(normed_item, weights, bias_table, head_loop)

    return run_items(single, (normed_low,), item_loop)


def section_backward(
    normed_low, upstream_low, weights, out_weight, bias_table, item_loop, head_loop
):

    def single(normed_item, upstream_item):
        return backward_item(normed_item, upstream_item, weights, out_weight, bias_table, head_loop)

    if bias_table is None:
        grad_proj, unused = run_items(single, (normed_low, upstream_low), item_loop)
        return (grad_proj, None)

    def accumulate(running, bundle):
        grad_proj, grad_scores = single(bundle[0], bundle[1])
        return (running + grad_scores, grad_proj)

    bias_total, grad_proj = lax.scan(
        accumulate, jnp.zeros(bias_table.shape, jnp.float32), (normed_low, upstream_low)
    )
    return (grad_proj, bias_total)


def column_block(columns, upstream, column_project, column_output, transition_in, transition_out):
    normed_cols, scale_cols = normalize(columns)
    normed_cols_low = normed_cols.astype(jnp.bfloat16)
    column_gated = section_forward(normed_cols_low, column_project, None, False, False)
    column_update = product("bhld,hdc->blc", column_gated, column_output.reshape(H, DH, C))
    after_columns = (columns.astype(jnp.float32) + column_update).astype(jnp.bfloat16)
    normed_two, scale_two = normalize(after_columns)
    normed_two_low = normed_two.astype(jnp.bfloat16)
    pre_hidden = product("blc,cfe->blfe", normed_two_low, transition_in)
    gate_part = pre_hidden[:, :, 0]
    up_part = pre_hidden[:, :, 1]
    sigmoid_gate = jax.nn.sigmoid(gate_part)
    activated = gate_part * sigmoid_gate
    hidden = (activated * up_part).astype(jnp.bfloat16)
    raw_trans_out = product("blf,blc->fc", hidden, upstream)
    grad_hidden = product("blc,fc->blf", upstream, transition_out)
    grad_gate_part = grad_hidden * up_part * sigmoid_gate * (1.0 + gate_part * (1.0 - sigmoid_gate))
    grad_up_part = grad_hidden * activated
    grad_pre = jnp.stack([grad_gate_part, grad_up_part], axis=2).astype(jnp.bfloat16)
    raw_trans_in = product("blc,blfe->cfe", normed_two_low, grad_pre)
    grad_normed_two = product("blfe,cfe->blc", grad_pre, transition_in)
    grad_after_columns = upstream.astype(jnp.float32) + norm_back(
        normed_two, scale_two, grad_normed_two
    )
    grad_columns_low = grad_after_columns.astype(jnp.bfloat16)
    grad_proj, unused = section_backward(
        normed_cols_low, grad_columns_low, column_project, column_output, None, False, False
    )
    raw_column_output = product("bhld,blc->hdc", column_gated, grad_columns_low).reshape(H * DH, C)
    raw_column_project = product("blc,bfhld->cfhd", normed_cols_low, grad_proj).reshape(
        C, 4, H * DH
    )
    grad_normed_cols = product("bfhld,cfhd->blc", grad_proj, column_project.reshape(C, 4, H, DH))
    grad_after_rows = (
        grad_after_columns + norm_back(normed_cols, scale_cols, grad_normed_cols)
    ).astype(jnp.bfloat16)
    return (grad_after_rows, raw_column_project, raw_column_output, raw_trans_in, raw_trans_out)


def row_block(
    normed_rows,
    scale_rows,
    normed_rows_low,
    row_gated,
    grad_after_rows,
    row_project,
    row_output,
    bias_table,
):
    grad_proj, bias_total = section_backward(
        normed_rows_low, grad_after_rows, row_project, row_output, bias_table, True, True
    )
    raw_row_output = product("bhld,blc->hdc", row_gated, grad_after_rows).reshape(H * DH, C)
    raw_row_project = product("blc,bfhld->cfhd", normed_rows_low, grad_proj).reshape(C, 4, H * DH)
    grad_normed_rows = product("bfhld,cfhd->blc", grad_proj, row_project.reshape(C, 4, H, DH))
    grad_alignment = (
        grad_after_rows.astype(jnp.float32) + norm_back(normed_rows, scale_rows, grad_normed_rows)
    ).astype(jnp.bfloat16)
    return (grad_alignment, raw_row_project, raw_row_output, bias_total)


def to_columns(arranged):
    moved = lax.all_to_all(arranged, ("dap", "sub"), split_axis=1, concat_axis=0, tiled=True)
    return moved


def to_rows(arranged):
    moved = lax.all_to_all(arranged, ("dap", "sub"), split_axis=0, concat_axis=1, tiled=True)
    return moved


def split_shards(
    alignment,
    pair_bias,
    row_project,
    row_output,
    column_project,
    column_output,
    transition_in,
    transition_out,
    cotangent,
):
    bias_full = lax.all_gather(pair_bias, ("dap", "sub"), axis=1, tiled=True)
    upstream = jnp.swapaxes(to_columns(cotangent), 0, 1)
    normed_rows, scale_rows = normalize(alignment)
    normed_rows_low = normed_rows.astype(jnp.bfloat16)
    row_gated = section_forward(normed_rows_low, row_project, bias_full, True, True)
    row_update = product("bhld,hdc->blc", row_gated, row_output.reshape(H, DH, C))
    after_rows = (alignment.astype(jnp.float32) + row_update).astype(jnp.bfloat16)
    columns = jnp.swapaxes(to_columns(after_rows), 0, 1)
    grad_columns, raw_column_project, raw_column_output, raw_trans_in, raw_trans_out = column_block(
        columns, upstream, column_project, column_output, transition_in, transition_out
    )
    sequences = alignment.shape[0] * lax.axis_size("dap") * lax.axis_size("sub")
    residues = alignment.shape[1]
    token_scale = (sequences * residues) ** (-0.5)
    term_col_project = raw_column_project * token_scale
    term_col_output = raw_column_output * token_scale
    term_trans_in = raw_trans_in * token_scale
    term_trans_out = raw_trans_out * token_scale
    grad_after_rows = to_rows(jnp.swapaxes(grad_columns, 0, 1))
    grad_alignment, raw_row_project, raw_row_output, bias_total = row_block(
        normed_rows,
        scale_rows,
        normed_rows_low,
        row_gated,
        grad_after_rows,
        row_project,
        row_output,
        bias_full,
    )
    term_row_project = raw_row_project * token_scale
    term_row_output = raw_row_output * token_scale
    bias_term = bias_total * (residues * sequences ** (-0.5))
    grad_bias = lax.psum_scatter(bias_term, ("dap", "sub"), scatter_dimension=1, tiled=True)
    (
        grad_row_project,
        grad_row_output,
        grad_col_project,
        grad_col_output,
        grad_trans_in,
        grad_trans_out,
    ) = (
        lax.psum_scatter(term_row_project, ("dap", "sub"), scatter_dimension=0, tiled=True),
        lax.psum_scatter(term_row_output, ("dap", "sub"), scatter_dimension=0, tiled=True),
        lax.psum_scatter(term_col_project, ("dap", "sub"), scatter_dimension=0, tiled=True),
        lax.psum_scatter(term_col_output, ("dap", "sub"), scatter_dimension=0, tiled=True),
        lax.psum_scatter(term_trans_in, ("dap", "sub"), scatter_dimension=0, tiled=True),
        lax.psum_scatter(term_trans_out, ("dap", "sub"), scatter_dimension=0, tiled=True),
    )
    return (
        grad_alignment,
        grad_bias,
        grad_row_project,
        grad_row_output,
        grad_col_project,
        grad_col_output,
        grad_trans_in,
        grad_trans_out,
    )


LANES = 128
ROWS = 16
BF = jnp.bfloat16
F32 = jnp.float32
MESH = pl.DeviceIdType.MESH


def dot(a, b, left=1, right=0, precision=None):
    return lax.dot_general(
        a, b, (((left,), (right,)), ((), ())), preferred_element_type=F32, precision=precision
    )


def iota(shape, axis):
    return lax.broadcasted_iota(jnp.int32, shape, axis)


def one_hot(condition):
    return jnp.where(condition, 1.0, 0.0).astype(BF)


def own_rows(me, rows, total):
    return one_hot(iota((rows, total), 1) == me * rows + iota((rows, total), 0))


def gang(nd, nz, oz, od):
    d, z = lax.axis_index("dap"), lax.axis_index("sub")
    return lax.rem(d + od, nd), lax.rem(z + oz, nz)


def send(buffer, slot, d, z, send_sem, recv_sem):
    return pltpu.make_async_remote_copy(
        src_ref=buffer.at[slot],
        dst_ref=buffer.at[slot],
        send_sem=send_sem,
        recv_sem=recv_sem,
        device_id={"dap": d, "sub": z},
        device_id_type=MESH,
    )


def spread_own(nd, nz, buffer, send_sem, recv_sem):
    me = lax.axis_index("dap") * nz + lax.axis_index("sub")
    copies = {}
    for oz in range(1, nz):
        d, z = gang(nd, nz, oz, 0)
        copies[oz, 0] = send(buffer, me, d, z, send_sem.at[oz, 0], recv_sem.at[oz, 0])
        copies[oz, 0].start()
    for od in range(1, nd):
        d, z = gang(nd, nz, 0, od)
        copies[0, od] = send(buffer, me, d, z, send_sem.at[0, od], recv_sem.at[0, od])
        copies[0, od].start()
    return copies


def relay(nd, nz, buffer, send_sem, recv_sem, copies):
    for oz in range(1, nz):
        copies[oz, 0].wait_recv()
        from_d, from_z = gang(nd, nz, nz - oz, 0)
        slot = from_d * nz + from_z
        for od in range(1, nd):
            d, z = gang(nd, nz, 0, od)
            copies[oz, od] = send(buffer, slot, d, z, send_sem.at[oz, od], recv_sem.at[oz, od])
            copies[oz, od].start()


def collect(copies):
    for (oz, od), copy in copies.items():
        if od:
            copy.wait_recv()


def head_mask(h, width):
    return one_hot(lax.div(iota((1, width), 1), DH) == h)


def stack_heads(rows):
    width = rows.shape[1]
    return jnp.concatenate([rows * head_mask(h, width) for h in range(H)], axis=0)


def merge_heads(stacked):
    width = stacked.shape[1]
    group = stacked.shape[0] // H
    lane_head = lax.div(iota((1, width), 1), DH)
    total = stacked[0:group]
    for h in range(1, H):
        total = jnp.where(lane_head == h, stacked[h * group : (h + 1) * group], total)
    return total


def block_mask(group, length):
    shape = (H * group, group)
    query = lax.rem(iota(shape, 0), group)
    return jnp.where(lax.div(query, length) == lax.div(iota(shape, 1), length), 0.0, -1e30)


def project(low, weight_ref):
    parts = [dot(low, weight_ref[f]) for f in range(4)]
    queries = (parts[0] * DH ** (-0.5)).astype(BF)
    return queries, parts[1].astype(BF), parts[2].astype(BF), jax.nn.sigmoid(parts[3])


def attend(queries, keys, values, extra, group, shares_ref):
    blended = []
    for g in range(queries.shape[0] // group):
        rows = slice(g * group, (g + 1) * group)
        scores = dot(stack_heads(queries[rows]), keys[rows], 1, 1) + extra
        powered = jnp.exp(scores - jnp.max(scores, axis=-1, keepdims=True))
        shares = powered * (1.0 / jnp.sum(powered, axis=-1, keepdims=True))
        shares_ref[g] = shares
        blended.append(merge_heads(dot(shares.astype(BF), values[rows])))
    return jnp.concatenate(blended, axis=0)


def attend_back(queries, keys, values, gating, blended, upstream, out_weight, group, shares_ref, score_sink):
    grad_gated = dot(upstream, out_weight, 1, 1)
    grad_blend = (grad_gated * gating).astype(BF)
    grads = ([], [], [])
    for g in range(queries.shape[0] // group):
        rows = slice(g * group, (g + 1) * group)
        shares = shares_ref[g]
        blend_stack = stack_heads(grad_blend[rows])
        grad_shares = dot(blend_stack, values[rows], 1, 1)
        centre = jnp.sum(shares * grad_shares, axis=-1, keepdims=True)
        grad_scores = shares * (grad_shares - centre)
        grad_low = grad_scores.astype(BF)
        if score_sink is not None:
            score_sink(grad_scores, grad_low)
        grads[0].append(merge_heads(dot(grad_low, keys[rows])) * DH ** (-0.5))
        grads[1].append(dot(grad_low, stack_heads(queries[rows]), 0, 0))
        grads[2].append(dot(shares.astype(BF), blend_stack, 0, 0))
    grad_gate = grad_gated * blended * gating * (1.0 - gating)
    parts = [jnp.concatenate(part, axis=0) for part in grads] + [grad_gate]
    return [part.astype(BF) for part in parts]


def sample_body(
    nd,
    nz,
    x_hbm,
    ct_hbm,
    bias_hbm,
    rp_hbm,
    ro_hbm,
    cp_hbm,
    co_hbm,
    ti_hbm,
    to_hbm,
    g_x,
    g_bias,
    g_rp,
    g_ro,
    g_cp,
    g_co,
    g_ti,
    g_to,
    x_in,
    ct_in,
    bias_in,
    x_all,
    ct_all,
    rp_in,
    ro_ref,
    cp_in,
    co_ref,
    ti_in,
    to_ref,
    rp_ref,
    cp_ref,
    ti_ref,
    row_shares,
    col_shares,
    load_sem,
    x_send,
    x_recv,
    ct_send,
    ct_recv,
):
    n = nd * nz
    me = lax.axis_index("dap") * nz + lax.axis_index("sub")
    barrier = pltpu.get_barrier_semaphore()
    for oz in range(nz):
        for od in range(nd):
            if (oz == 0) != (od == 0):
                d, z = gang(nd, nz, oz, od)
                pl.semaphore_signal(
                    barrier, inc=1, device_id={"dap": d, "sub": z}, device_id_type=MESH
                )
    sources = (x_hbm, bias_hbm, ct_hbm, rp_hbm, cp_hbm, ti_hbm, ro_hbm, co_hbm, to_hbm)
    targets = (x_in, bias_in, ct_in, rp_in, cp_in, ti_in, ro_ref, co_ref, to_ref)
    loads = [
        pltpu.make_async_copy(source, target, load_sem.at[i])
        for i, (source, target) in enumerate(zip(sources, targets))
    ]
    for load in loads:
        load.start()
    for load in loads[:3]:
        load.wait()
    loads = loads[3:]
    residues = x_in.shape[0]
    seqs = n
    tokens = seqs * residues
    group = LANES
    scale = tokens ** (-0.5)
    spread = one_hot(lax.rem(iota((residues, LANES), 1), residues) == iota((residues, LANES), 0))
    tiled = dot(bias_in[...], spread)
    padded = jnp.concatenate([tiled, jnp.zeros((ROWS - H, LANES), F32)], axis=0).astype(BF)
    x_all[me, :, 0:C] = x_in[...]
    x_all[me, 0:ROWS, C : C + LANES] = padded
    ct_all[me] = ct_in[...]
    pl.semaphore_wait(barrier, nz + nd - 2)
    x_copies = spread_own(nd, nz, x_all, x_send, x_recv)
    ct_copies = spread_own(nd, nz, ct_all, ct_send, ct_recv)
    relay(nd, nz, x_all, x_send, x_recv, x_copies)
    loads[0].wait()
    for f in range(4):
        rp_ref[f] = rp_in[:, f, :]
    loads[1].wait()
    for f in range(4):
        cp_ref[f] = cp_in[:, f, :]
    relay(nd, nz, ct_all, ct_send, ct_recv, ct_copies)
    loads[2].wait()
    for f in range(2):
        ti_ref[f] = ti_in[:, f, :]
    for load in loads[3:]:
        load.wait()
    collect(x_copies)

    x = x_all[:, :, 0:C].reshape(tokens, C)
    bias_rows = x_all[:, 0:ROWS, C : C + LANES].reshape(n * ROWS, LANES)

    shape = (H * group, n * ROWS)
    row_at, col_at = iota(shape, 0), iota(shape, 1)
    pick = one_hot(
        (lax.div(col_at, ROWS) == lax.rem(row_at, residues))
        & (lax.rem(col_at, ROWS) == lax.div(row_at, group))
    )
    row_extra = dot(pick, bias_rows) + block_mask(group, residues)
    col_extra = block_mask(group, seqs)

    rows_f, scale_rows = normalize(x)
    rows_low = rows_f.astype(BF)
    rq, rk, rv, rgate = project(rows_low, rp_ref)
    rblend = attend(rq, rk, rv, row_extra, group, row_shares)
    row_gated = (rblend * rgate).astype(BF)
    after_rows = (x.astype(F32) + dot(row_gated, ro_ref[...])).astype(BF)

    square = (tokens, tokens)
    to_cols = one_hot(
        iota(square, 1) == lax.rem(iota(square, 0), seqs) * residues + lax.div(iota(square, 0), seqs)
    )
    columns = dot(to_cols, after_rows).astype(BF)

    cols_f, scale_cols = normalize(columns)
    cols_low = cols_f.astype(BF)
    cq, ck, cv, cgate = project(cols_low, cp_ref)
    cblend = attend(cq, ck, cv, col_extra, group, col_shares)
    col_gated = (cblend * cgate).astype(BF)
    after_cols = (columns.astype(F32) + dot(col_gated, co_ref[...])).astype(BF)

    collect(ct_copies)
    ct = ct_all[...].reshape(tokens, C)
    upstream = dot(to_cols, ct).astype(BF)

    two_f, scale_two = normalize(after_cols)
    two_low = two_f.astype(BF)
    own_c = own_rows(me, C // n, C)
    two_own = dot(own_c, two_low, 1, 1).astype(BF)
    hidden_units = to_ref.shape[0]
    own_f = hidden_units // n
    chunk = C
    grad_two = None
    hidden_own = None
    for at in range(0, hidden_units, chunk):
        piece = slice(at, at + chunk)
        gate_part = dot(two_low, ti_ref[0, :, piece])
        up_part = dot(two_low, ti_ref[1, :, piece])
        sigmoid_gate = jax.nn.sigmoid(gate_part)
        activated = gate_part * sigmoid_gate
        hidden = (activated * up_part).astype(BF)
        select = one_hot(iota((own_f, chunk), 1) + at == me * own_f + iota((own_f, chunk), 0))
        held = dot(select, hidden, 1, 1)
        hidden_own = held if hidden_own is None else hidden_own + held
        grad_hidden = dot(upstream, to_ref[piece, :], 1, 1)
        grad_gate_part = (
            grad_hidden * up_part * sigmoid_gate * (1.0 + gate_part * (1.0 - sigmoid_gate))
        ).astype(BF)
        grad_up_part = (grad_hidden * activated).astype(BF)
        g_ti[:, 0, piece] = dot(two_own, grad_gate_part) * scale
        g_ti[:, 1, piece] = dot(two_own, grad_up_part) * scale
        part = dot(grad_gate_part, ti_ref[0, :, piece], 1, 1) + dot(
            grad_up_part, ti_ref[1, :, piece], 1, 1
        )
        grad_two = part if grad_two is None else grad_two + part
    g_to[...] = dot(hidden_own.astype(BF), upstream) * scale
    grad_after_cols = upstream.astype(F32) + norm_back(two_f, scale_two, grad_two)
    grad_cols_low = grad_after_cols.astype(BF)

    col_grads = attend_back(
        cq, ck, cv, cgate, cblend, grad_cols_low, co_ref[...], group, col_shares, None
    )
    g_co[...] = dot(dot(own_c, col_gated, 1, 1).astype(BF), grad_cols_low) * scale
    cols_own = dot(own_c, cols_low, 1, 1).astype(BF)
    grad_cols = None
    for f in range(4):
        g_cp[:, f, :] = dot(cols_own, col_grads[f]) * scale
        part = dot(col_grads[f], cp_ref[f], 1, 1)
        grad_cols = part if grad_cols is None else grad_cols + part
    grad_rows_cols = (grad_after_cols + norm_back(cols_f, scale_cols, grad_cols)).astype(BF)

    to_rows_hot = one_hot(
        iota(square, 1)
        == lax.rem(iota(square, 0), residues) * seqs + lax.div(iota(square, 0), residues)
    )
    grad_rows = dot(to_rows_hot, grad_rows_cols).astype(BF)

    bias_shape = (H, H * group)
    at_head, at_row = iota(bias_shape, 0), iota(bias_shape, 1)
    bias_pick = one_hot(
        (lax.div(at_row, group) == at_head) & (lax.rem(at_row, residues) == me)
    )
    bias_sums = []

    def sink(grad_scores, grad_low):
        rest = (grad_scores - grad_low.astype(F32)).astype(BF)
        bias_sums.append(dot(bias_pick, grad_low) + dot(bias_pick, rest))

    row_grads = attend_back(
        rq, rk, rv, rgate, rblend, grad_rows, ro_ref[...], group, row_shares, sink
    )
    bias_sum = bias_sums[0]
    for more in bias_sums[1:]:
        bias_sum = bias_sum + more
    folded = bias_sum[:, 0:residues]
    for at in range(residues, group, residues):
        folded = folded + bias_sum[:, at : at + residues]
    g_bias[:, 0, :] = folded * (residues * seqs ** (-0.5))

    g_ro[...] = dot(dot(own_c, row_gated, 1, 1).astype(BF), grad_rows) * scale
    rows_own = dot(own_c, rows_low, 1, 1).astype(BF)
    own_t = own_rows(me, residues, tokens)
    grad_own = None
    for f in range(4):
        g_rp[:, f, :] = dot(rows_own, row_grads[f]) * scale
        part = dot(dot(own_t, row_grads[f]).astype(BF), rp_ref[f], 1, 1)
        grad_own = part if grad_own is None else grad_own + part
    x_own, scale_own = normalize(x_in[...])
    g_x[...] = (dot(own_t, grad_rows) + norm_back(x_own, scale_own, grad_own)).astype(BF)
    for copy in list(x_copies.values()) + list(ct_copies.values()):
        copy.wait_send()


def hand_over(*refs):
    count = (len(refs) - 1) // 2
    copies = [
        pltpu.make_async_copy(refs[i], refs[count + i], refs[-1].at[i]) for i in range(count)
    ]
    for copy in copies:
        copy.start()
    for copy in copies:
        copy.wait()


def whole_shards(
    alignment,
    pair_bias,
    row_project,
    row_output,
    column_project,
    column_output,
    transition_in,
    transition_out,
    cotangent,
):
    nd, nz = lax.axis_size("dap"), lax.axis_size("sub")
    n = nd * nz
    residues = alignment.shape[1]
    tokens = n * residues
    vmem = pl.BlockSpec(memory_space=pltpu.VMEM)
    hbm = pl.BlockSpec(memory_space=pltpu.HBM)
    hidden_units = transition_out.shape[0]
    outs = (
        jax.ShapeDtypeStruct((residues, C), BF),
        jax.ShapeDtypeStruct((H, 1, residues), F32),
        jax.ShapeDtypeStruct((C // n, 4, H * DH), F32),
        jax.ShapeDtypeStruct((H * DH // n, C), F32),
        jax.ShapeDtypeStruct((C // n, 4, H * DH), F32),
        jax.ShapeDtypeStruct((H * DH // n, C), F32),
        jax.ShapeDtypeStruct((C // n, 2, hidden_units), F32),
        jax.ShapeDtypeStruct((hidden_units // n, C), F32),
    )
    weights = (
        row_project,
        row_output,
        column_project,
        column_output,
        transition_in,
        transition_out,
    )
    results = pl.pallas_call(
        functools.partial(sample_body, nd, nz),
        out_shape=outs,
        in_specs=[hbm] * 9,
        out_specs=(vmem,) * 8,
        scratch_shapes=[
            pltpu.VMEM((residues, C), BF),
            pltpu.VMEM((residues, C), BF),
            pltpu.VMEM((H, residues), BF),
            pltpu.VMEM((n, residues, C + LANES), BF),
            pltpu.VMEM((n, residues, C), BF),
        ]
        + [pltpu.VMEM(weight.shape, BF) for weight in weights]
        + [
            pltpu.VMEM((4, C, H * DH), BF),
            pltpu.VMEM((4, C, H * DH), BF),
            pltpu.VMEM((2, C, hidden_units), BF),
            pltpu.VMEM((tokens // LANES, H * LANES, LANES), F32),
            pltpu.VMEM((tokens // LANES, H * LANES, LANES), F32),
            pltpu.SemaphoreType.DMA((len(weights) + 3,)),
        ]
        + [pltpu.SemaphoreType.DMA((nz, nd))] * 4,
        compiler_params=pltpu.CompilerParams(
            collective_id=0, has_side_effects=True, vmem_limit_bytes=63 * 1024 * 1024
        ),
        name="sample_backward",
    )(
        alignment.reshape(residues, C),
        cotangent.reshape(residues, C),
        pair_bias.reshape(H, residues),
        *weights,
    )
    results = pl.pallas_call(
        hand_over,
        out_shape=outs,
        in_specs=[pl.BlockSpec(memory_space=pl.ANY)] * len(outs),
        out_specs=(hbm,) * len(outs),
        scratch_shapes=[pltpu.SemaphoreType.DMA((len(outs),))],
        name="hand_over",
    )(*results)
    return (results[0].reshape(alignment.shape),) + tuple(results[1:])


def shards(alignment, pair_bias, *rest):
    n = lax.axis_size("dap") * lax.axis_size("sub")
    residues = alignment.shape[1]
    tokens = alignment.shape[0] * n * residues
    fits = (
        alignment.shape[0] == 1
        and pair_bias.shape[1] == 1
        and residues >= ROWS
        and residues % ROWS == 0
        and H <= ROWS
        and LANES % residues == 0
        and LANES % n == 0
        and tokens % LANES == 0
        and tokens <= 4 * LANES
    )
    if fits:
        return whole_shards(alignment, pair_bias, *rest)
    return split_shards(alignment, pair_bias, *rest)


def solution(mesh):
    in_specs = (
        P(("grp", "dap", "sub"), None, None),
        P(None, ("grp", "dap", "sub"), None),
        P(),
        P(),
        P(),
        P(),
        P(),
        P(),
        P(("grp", "dap", "sub"), None, None),
    )
    out_specs = (
        P(("grp", "dap", "sub"), None, None),
        P(None, ("grp", "dap", "sub"), None),
        P(("grp", "dap", "sub"), None, None),
        P(("grp", "dap", "sub"), None),
        P(("grp", "dap", "sub"), None, None),
        P(("grp", "dap", "sub"), None),
        P(("grp", "dap", "sub"), None, None),
        P(("grp", "dap", "sub"), None),
    )
    return jax.shard_map(shards, mesh=mesh, in_specs=in_specs, out_specs=out_specs, check_vma=False)
```

```python
import jax
import jax.numpy as jnp
from jax import lax
from jax.experimental import pallas as pl
from jax.experimental.pallas import tpu as pltpu
from jax.sharding import PartitionSpec as P
import functools

C = 256
H = 8
DH = 32


EPSILON = 1e-05


def product(pattern, former, latter):
    return jnp.einsum(pattern, former, latter, preferred_element_type=jnp.float32)


def normalize(values):
    values = values.astype(jnp.float32)
    centred = values - jnp.mean(values, axis=-1, keepdims=True)
    factor = lax.rsqrt(jnp.mean(centred * centred, axis=-1, keepdims=True) + EPSILON)
    return (centred * factor, factor)


def norm_back(normed, factor, upstream):
    mean_up = jnp.mean(upstream, axis=-1, keepdims=True)
    mean_cross = jnp.mean(upstream * normed, axis=-1, keepdims=True)
    return factor * (upstream - mean_up - normed * mean_cross)


def run_items(function, arrays, sequential):
    if sequential:
        return lax.map(lambda bundle: function(*bundle), arrays)
    return jax.vmap(function)(*arrays)


def head_shares(queries, key_rows, bias_head):
    scores = product("qd,kd->qk", queries, key_rows)
    if bias_head is not None:
        scores = scores + bias_head.astype(jnp.float32)
    row_top = jnp.max(scores, axis=-1, keepdims=True)
    powered = jnp.exp(scores - row_top)
    return powered / jnp.sum(powered, axis=-1, keepdims=True)


def head_forward(queries, key_rows, values, bias_head=None):
    shares = head_shares(queries, key_rows, bias_head)
    return product("qk,kd->qd", shares.astype(jnp.bfloat16), values)


def head_backward(queries, key_rows, values, grad_blend, bias_head=None):
    shares = head_shares(queries, key_rows, bias_head)
    shares_low = shares.astype(jnp.bfloat16)
    blended = product("qk,kd->qd", shares_low, values)
    grad_shares = product("qd,kd->qk", grad_blend, values)
    grad_values = product("qk,qd->kd", shares_low, grad_blend)
    centre = jnp.sum(shares * grad_shares, axis=-1, keepdims=True)
    grad_scores = shares * (grad_shares - centre)
    grad_low = grad_scores.astype(jnp.bfloat16)
    grad_queries = product("qk,kd->qd", grad_low, key_rows)
    grad_keys = product("qk,qd->kd", grad_low, queries)
    return (blended, grad_queries, grad_keys, grad_values, grad_scores)


def item_project(normed_item, weights):
    projected = product("lc,cfhd->fhld", normed_item, weights.reshape(C, 4, H, DH))
    queries = (projected[0] * DH ** (-0.5)).astype(jnp.bfloat16)
    key_rows = projected[1].astype(jnp.bfloat16)
    values = projected[2].astype(jnp.bfloat16)
    gating = jax.nn.sigmoid(projected[3])
    return (queries, key_rows, values, gating)


def forward_item(normed_item, weights, bias_table, head_loop):
    queries, key_rows, values, gating = item_project(normed_item, weights)
    if bias_table is None:
        head_args = (queries, key_rows, values)
    else:
        head_args = (queries, key_rows, values, bias_table)
    blended = run_items(head_forward, head_args, head_loop)
    return (blended * gating).astype(jnp.bfloat16)


def backward_item(normed_item, upstream_item, weights, out_weight, bias_table, head_loop):
    queries, key_rows, values, gating = item_project(normed_item, weights)
    grad_gated = product("lc,hdc->hld", upstream_item, out_weight.reshape(H, DH, C))
    grad_blend = (grad_gated * gating).astype(jnp.bfloat16)
    if bias_table is None:
        head_args = (queries, key_rows, values, grad_blend)
    else:
        head_args = (queries, key_rows, values, grad_blend, bias_table)
    blended, grad_queries, grad_keys, grad_values, grad_scores = run_items(
        head_backward, head_args, head_loop
    )
    grad_gate = grad_gated * blended * gating * (1.0 - gating)
    grad_proj = jnp.stack(
        [grad_queries * DH ** (-0.5), grad_keys, grad_values, grad_gate], axis=0
    ).astype(jnp.bfloat16)
    if bias_table is None:
        return (grad_proj, jnp.zeros((), jnp.float32))
    return (grad_proj, grad_scores)


def section_forward(normed_low, weights, bias_table, item_loop, head_loop):

    def single(normed_item):
        return forward_item(normed_item, weights, bias_table, head_loop)

    return run_items(single, (normed_low,), item_loop)


def section_backward(
    normed_low, upstream_low, weights, out_weight, bias_table, item_loop, head_loop
):

    def single(normed_item, upstream_item):
        return backward_item(normed_item, upstream_item, weights, out_weight, bias_table, head_loop)

    if bias_table is None:
        grad_proj, unused = run_items(single, (normed_low, upstream_low), item_loop)
        return (grad_proj, None)

    def accumulate(running, bundle):
        grad_proj, grad_scores = single(bundle[0], bundle[1])
        return (running + grad_scores, grad_proj)

    bias_total, grad_proj = lax.scan(
        accumulate, jnp.zeros(bias_table.shape, jnp.float32), (normed_low, upstream_low)
    )
    return (grad_proj, bias_total)


def column_block(columns, upstream, column_project, column_output, transition_in, transition_out):
    normed_cols, scale_cols = normalize(columns)
    normed_cols_low = normed_cols.astype(jnp.bfloat16)
    column_gated = section_forward(normed_cols_low, column_project, None, False, False)
    column_update = product("bhld,hdc->blc", column_gated, column_output.reshape(H, DH, C))
    after_columns = (columns.astype(jnp.float32) + column_update).astype(jnp.bfloat16)
    normed_two, scale_two = normalize(after_columns)
    normed_two_low = normed_two.astype(jnp.bfloat16)
    pre_hidden = product("blc,cfe->blfe", normed_two_low, transition_in)
    gate_part = pre_hidden[:, :, 0]
    up_part = pre_hidden[:, :, 1]
    sigmoid_gate = jax.nn.sigmoid(gate_part)
    activated = gate_part * sigmoid_gate
    hidden = (activated * up_part).astype(jnp.bfloat16)
    raw_trans_out = product("blf,blc->fc", hidden, upstream)
    grad_hidden = product("blc,fc->blf", upstream, transition_out)
    grad_gate_part = grad_hidden * up_part * sigmoid_gate * (1.0 + gate_part * (1.0 - sigmoid_gate))
    grad_up_part = grad_hidden * activated
    grad_pre = jnp.stack([grad_gate_part, grad_up_part], axis=2).astype(jnp.bfloat16)
    raw_trans_in = product("blc,blfe->cfe", normed_two_low, grad_pre)
    grad_normed_two = product("blfe,cfe->blc", grad_pre, transition_in)
    grad_after_columns = upstream.astype(jnp.float32) + norm_back(
        normed_two, scale_two, grad_normed_two
    )
    grad_columns_low = grad_after_columns.astype(jnp.bfloat16)
    grad_proj, unused = section_backward(
        normed_cols_low, grad_columns_low, column_project, column_output, None, False, False
    )
    raw_column_output = product("bhld,blc->hdc", column_gated, grad_columns_low).reshape(H * DH, C)
    raw_column_project = product("blc,bfhld->cfhd", normed_cols_low, grad_proj).reshape(
        C, 4, H * DH
    )
    grad_normed_cols = product("bfhld,cfhd->blc", grad_proj, column_project.reshape(C, 4, H, DH))
    grad_after_rows = (
        grad_after_columns + norm_back(normed_cols, scale_cols, grad_normed_cols)
    ).astype(jnp.bfloat16)
    return (grad_after_rows, raw_column_project, raw_column_output, raw_trans_in, raw_trans_out)


def row_block(
    normed_rows,
    scale_rows,
    normed_rows_low,
    row_gated,
    grad_after_rows,
    row_project,
    row_output,
    bias_table,
):
    grad_proj, bias_total = section_backward(
        normed_rows_low, grad_after_rows, row_project, row_output, bias_table, True, True
    )
    raw_row_output = product("bhld,blc->hdc", row_gated, grad_after_rows).reshape(H * DH, C)
    raw_row_project = product("blc,bfhld->cfhd", normed_rows_low, grad_proj).reshape(C, 4, H * DH)
    grad_normed_rows = product("bfhld,cfhd->blc", grad_proj, row_project.reshape(C, 4, H, DH))
    grad_alignment = (
        grad_after_rows.astype(jnp.float32) + norm_back(normed_rows, scale_rows, grad_normed_rows)
    ).astype(jnp.bfloat16)
    return (grad_alignment, raw_row_project, raw_row_output, bias_total)


def to_columns(arranged):
    moved = lax.all_to_all(arranged, ("dap", "sub"), split_axis=1, concat_axis=0, tiled=True)
    return moved


def to_rows(arranged):
    moved = lax.all_to_all(arranged, ("dap", "sub"), split_axis=0, concat_axis=1, tiled=True)
    return moved


def split_shards(
    alignment,
    pair_bias,
    row_project,
    row_output,
    column_project,
    column_output,
    transition_in,
    transition_out,
    cotangent,
):
    bias_full = lax.all_gather(pair_bias, ("dap", "sub"), axis=1, tiled=True)
    upstream = jnp.swapaxes(to_columns(cotangent), 0, 1)
    normed_rows, scale_rows = normalize(alignment)
    normed_rows_low = normed_rows.astype(jnp.bfloat16)
    row_gated = section_forward(normed_rows_low, row_project, bias_full, True, True)
    row_update = product("bhld,hdc->blc", row_gated, row_output.reshape(H, DH, C))
    after_rows = (alignment.astype(jnp.float32) + row_update).astype(jnp.bfloat16)
    columns = jnp.swapaxes(to_columns(after_rows), 0, 1)
    grad_columns, raw_column_project, raw_column_output, raw_trans_in, raw_trans_out = column_block(
        columns, upstream, column_project, column_output, transition_in, transition_out
    )
    sequences = alignment.shape[0] * lax.axis_size("dap") * lax.axis_size("sub")
    residues = alignment.shape[1]
    token_scale = (sequences * residues) ** (-0.5)
    term_col_project = raw_column_project * token_scale
    term_col_output = raw_column_output * token_scale
    term_trans_in = raw_trans_in * token_scale
    term_trans_out = raw_trans_out * token_scale
    grad_after_rows = to_rows(jnp.swapaxes(grad_columns, 0, 1))
    grad_alignment, raw_row_project, raw_row_output, bias_total = row_block(
        normed_rows,
        scale_rows,
        normed_rows_low,
        row_gated,
        grad_after_rows,
        row_project,
        row_output,
        bias_full,
    )
    term_row_project = raw_row_project * token_scale
    term_row_output = raw_row_output * token_scale
    bias_term = bias_total * (residues * sequences ** (-0.5))
    grad_bias = lax.psum_scatter(bias_term, ("dap", "sub"), scatter_dimension=1, tiled=True)
    (
        grad_row_project,
        grad_row_output,
        grad_col_project,
        grad_col_output,
        grad_trans_in,
        grad_trans_out,
    ) = (
        lax.psum_scatter(term_row_project, ("dap", "sub"), scatter_dimension=0, tiled=True),
        lax.psum_scatter(term_row_output, ("dap", "sub"), scatter_dimension=0, tiled=True),
        lax.psum_scatter(term_col_project, ("dap", "sub"), scatter_dimension=0, tiled=True),
        lax.psum_scatter(term_col_output, ("dap", "sub"), scatter_dimension=0, tiled=True),
        lax.psum_scatter(term_trans_in, ("dap", "sub"), scatter_dimension=0, tiled=True),
        lax.psum_scatter(term_trans_out, ("dap", "sub"), scatter_dimension=0, tiled=True),
    )
    return (
        grad_alignment,
        grad_bias,
        grad_row_project,
        grad_row_output,
        grad_col_project,
        grad_col_output,
        grad_trans_in,
        grad_trans_out,
    )


LANES = 128
ROWS = 16
BF = jnp.bfloat16
F32 = jnp.float32
MESH = pl.DeviceIdType.MESH


def dot(a, b, left=1, right=0, precision=None):
    return lax.dot_general(
        a, b, (((left,), (right,)), ((), ())), preferred_element_type=F32, precision=precision
    )


def iota(shape, axis):
    return lax.broadcasted_iota(jnp.int32, shape, axis)


def one_hot(condition):
    return jnp.where(condition, 1.0, 0.0).astype(BF)


def own_rows(me, rows, total):
    return one_hot(iota((rows, total), 1) == me * rows + iota((rows, total), 0))


def gang(nd, nz, oz, od):
    d, z = lax.axis_index("dap"), lax.axis_index("sub")
    return lax.rem(d + od, nd), lax.rem(z + oz, nz)


def send(buffer, slot, d, z, send_sem, recv_sem):
    return pltpu.make_async_remote_copy(
        src_ref=buffer.at[slot],
        dst_ref=buffer.at[slot],
        send_sem=send_sem,
        recv_sem=recv_sem,
        device_id={"dap": d, "sub": z},
        device_id_type=MESH,
    )


def spread_own(nd, nz, buffer, send_sem, recv_sem):
    me = lax.axis_index("dap") * nz + lax.axis_index("sub")
    copies = {}
    for oz in range(1, nz):
        d, z = gang(nd, nz, oz, 0)
        copies[oz, 0] = send(buffer, me, d, z, send_sem.at[oz, 0], recv_sem.at[oz, 0])
        copies[oz, 0].start()
    for od in range(1, nd):
        d, z = gang(nd, nz, 0, od)
        copies[0, od] = send(buffer, me, d, z, send_sem.at[0, od], recv_sem.at[0, od])
        copies[0, od].start()
    return copies


def relay(nd, nz, buffer, send_sem, recv_sem, copies):
    for oz in range(1, nz):
        copies[oz, 0].wait_recv()
        from_d, from_z = gang(nd, nz, nz - oz, 0)
        slot = from_d * nz + from_z
        for od in range(1, nd):
            d, z = gang(nd, nz, 0, od)
            copies[oz, od] = send(buffer, slot, d, z, send_sem.at[oz, od], recv_sem.at[oz, od])
            copies[oz, od].start()


def collect(copies):
    for (oz, od), copy in copies.items():
        if od:
            copy.wait_recv()


def head_mask(h, width):
    return one_hot(lax.div(iota((1, width), 1), DH) == h)


def stack_heads(rows):
    width = rows.shape[1]
    return jnp.concatenate([rows * head_mask(h, width) for h in range(H)], axis=0)


def merge_heads(stacked):
    width = stacked.shape[1]
    group = stacked.shape[0] // H
    lane_head = lax.div(iota((1, width), 1), DH)
    total = stacked[0:group]
    for h in range(1, H):
        total = jnp.where(lane_head == h, stacked[h * group : (h + 1) * group], total)
    return total


def block_mask(group, length):
    shape = (H * group, group)
    query = lax.rem(iota(shape, 0), group)
    return jnp.where(lax.div(query, length) == lax.div(iota(shape, 1), length), 0.0, -1e30)


def project(low, weight_ref):
    parts = [dot(low, weight_ref[f]) for f in range(4)]
    queries = (parts[0] * DH ** (-0.5)).astype(BF)
    return queries, parts[1].astype(BF), parts[2].astype(BF), jax.nn.sigmoid(parts[3])


def attend(queries, keys, values, extra, group, shares_ref):
    blended = []
    for g in range(queries.shape[0] // group):
        rows = slice(g * group, (g + 1) * group)
        scores = dot(stack_heads(queries[rows]), keys[rows], 1, 1) + extra
        powered = jnp.exp(scores - jnp.max(scores, axis=-1, keepdims=True))
        shares = powered * (1.0 / jnp.sum(powered, axis=-1, keepdims=True))
        shares_ref[g] = shares
        blended.append(merge_heads(dot(shares.astype(BF), values[rows])))
    return jnp.concatenate(blended, axis=0)


def attend_back(queries, keys, values, gating, blended, upstream, out_weight, group, shares_ref, score_sink):
    grad_gated = dot(upstream, out_weight, 1, 1)
    grad_blend = (grad_gated * gating).astype(BF)
    grads = ([], [], [])
    for g in range(queries.shape[0] // group):
        rows = slice(g * group, (g + 1) * group)
        shares = shares_ref[g]
        blend_stack = stack_heads(grad_blend[rows])
        grad_shares = dot(blend_stack, values[rows], 1, 1)
        centre = jnp.sum(shares * grad_shares, axis=-1, keepdims=True)
        grad_scores = shares * (grad_shares - centre)
        grad_low = grad_scores.astype(BF)
        if score_sink is not None:
            score_sink(grad_scores, grad_low)
        grads[0].append(merge_heads(dot(grad_low, keys[rows])) * DH ** (-0.5))
        grads[1].append(dot(grad_low, stack_heads(queries[rows]), 0, 0))
        grads[2].append(dot(shares.astype(BF), blend_stack, 0, 0))
    grad_gate = grad_gated * blended * gating * (1.0 - gating)
    parts = [jnp.concatenate(part, axis=0) for part in grads] + [grad_gate]
    return [part.astype(BF) for part in parts]


def sample_body(
    nd,
    nz,
    x_hbm,
    ct_hbm,
    bias_hbm,
    rp_hbm,
    ro_hbm,
    cp_hbm,
    co_hbm,
    ti_hbm,
    to_hbm,
    g_x,
    g_bias,
    g_rp,
    g_ro,
    g_cp,
    g_co,
    g_ti,
    g_to,
    x_in,
    ct_in,
    bias_in,
    x_all,
    ct_all,
    rp_in,
    ro_ref,
    cp_in,
    co_ref,
    ti_in,
    to_ref,
    rp_ref,
    cp_ref,
    ti_ref,
    row_shares,
    col_shares,
    load_sem,
    x_send,
    x_recv,
    ct_send,
    ct_recv,
):
    n = nd * nz
    me = lax.axis_index("dap") * nz + lax.axis_index("sub")
    barrier = pltpu.get_barrier_semaphore()
    for oz in range(nz):
        for od in range(nd):
            if (oz == 0) != (od == 0):
                d, z = gang(nd, nz, oz, od)
                pl.semaphore_signal(
                    barrier, inc=1, device_id={"dap": d, "sub": z}, device_id_type=MESH
                )
    sources = (x_hbm, bias_hbm, ct_hbm, rp_hbm, cp_hbm, ti_hbm, ro_hbm, co_hbm, to_hbm)
    targets = (x_in, bias_in, ct_in, rp_in, cp_in, ti_in, ro_ref, co_ref, to_ref)
    loads = [
        pltpu.make_async_copy(source, target, load_sem.at[i])
        for i, (source, target) in enumerate(zip(sources, targets))
    ]
    for load in loads:
        load.start()
    for load in loads[:3]:
        load.wait()
    loads = loads[3:]
    residues = x_in.shape[0]
    seqs = n
    tokens = seqs * residues
    group = LANES
    scale = tokens ** (-0.5)
    spread = one_hot(lax.rem(iota((residues, LANES), 1), residues) == iota((residues, LANES), 0))
    tiled = dot(bias_in[...], spread)
    padded = jnp.concatenate([tiled, jnp.zeros((ROWS - H, LANES), F32)], axis=0).astype(BF)
    x_all[me, :, 0:C] = x_in[...]
    x_all[me, 0:ROWS, C : C + LANES] = padded
    ct_all[me] = ct_in[...]
    pl.semaphore_wait(barrier, nz + nd - 2)
    x_copies = spread_own(nd, nz, x_all, x_send, x_recv)
    ct_copies = spread_own(nd, nz, ct_all, ct_send, ct_recv)
    relay(nd, nz, x_all, x_send, x_recv, x_copies)
    loads[0].wait()
    for f in range(4):
        rp_ref[f] = rp_in[:, f, :]
    loads[1].wait()
    for f in range(4):
        cp_ref[f] = cp_in[:, f, :]
    relay(nd, nz, ct_all, ct_send, ct_recv, ct_copies)
    loads[2].wait()
    for f in range(2):
        ti_ref[f] = ti_in[:, f, :]
    for load in loads[3:]:
        load.wait()
    collect(x_copies)

    x = x_all[:, :, 0:C].reshape(tokens, C)
    bias_rows = x_all[:, 0:ROWS, C : C + LANES].reshape(n * ROWS, LANES)

    shape = (H * group, n * ROWS)
    row_at, col_at = iota(shape, 0), iota(shape, 1)
    pick = one_hot(
        (lax.div(col_at, ROWS) == lax.rem(row_at, residues))
        & (lax.rem(col_at, ROWS) == lax.div(row_at, group))
    )
    row_extra = dot(pick, bias_rows) + block_mask(group, residues)
    col_extra = block_mask(group, seqs)

    rows_f, scale_rows = normalize(x)
    rows_low = rows_f.astype(BF)
    rq, rk, rv, rgate = project(rows_low, rp_ref)
    rblend = attend(rq, rk, rv, row_extra, group, row_shares)
    row_gated = (rblend * rgate).astype(BF)
    after_rows = (x.astype(F32) + dot(row_gated, ro_ref[...])).astype(BF)

    square = (tokens, tokens)
    to_cols = one_hot(
        iota(square, 1) == lax.rem(iota(square, 0), seqs) * residues + lax.div(iota(square, 0), seqs)
    )
    columns = dot(to_cols, after_rows).astype(BF)

    cols_f, scale_cols = normalize(columns)
    cols_low = cols_f.astype(BF)
    cq, ck, cv, cgate = project(cols_low, cp_ref)
    cblend = attend(cq, ck, cv, col_extra, group, col_shares)
    col_gated = (cblend * cgate).astype(BF)
    after_cols = (columns.astype(F32) + dot(col_gated, co_ref[...])).astype(BF)

    collect(ct_copies)
    ct = ct_all[...].reshape(tokens, C)
    upstream = dot(to_cols, ct).astype(BF)

    two_f, scale_two = normalize(after_cols)
    two_low = two_f.astype(BF)
    own_c = own_rows(me, C // n, C)
    two_own = dot(own_c, two_low, 1, 1).astype(BF)
    hidden_units = to_ref.shape[0]
    own_f = hidden_units // n
    chunk = C
    grad_two = None
    hidden_own = None
    for at in range(0, hidden_units, chunk):
        piece = slice(at, at + chunk)
        gate_part = dot(two_low, ti_ref[0, :, piece])
        up_part = dot(two_low, ti_ref[1, :, piece])
        sigmoid_gate = jax.nn.sigmoid(gate_part)
        activated = gate_part * sigmoid_gate
        hidden = (activated * up_part).astype(BF)
        select = one_hot(iota((own_f, chunk), 1) + at == me * own_f + iota((own_f, chunk), 0))
        held = dot(select, hidden, 1, 1)
        hidden_own = held if hidden_own is None else hidden_own + held
        grad_hidden = dot(upstream, to_ref[piece, :], 1, 1)
        grad_gate_part = (
            grad_hidden * up_part * sigmoid_gate * (1.0 + gate_part * (1.0 - sigmoid_gate))
        ).astype(BF)
        grad_up_part = (grad_hidden * activated).astype(BF)
        g_ti[:, 0, piece] = dot(two_own, grad_gate_part) * scale
        g_ti[:, 1, piece] = dot(two_own, grad_up_part) * scale
        part = dot(grad_gate_part, ti_ref[0, :, piece], 1, 1) + dot(
            grad_up_part, ti_ref[1, :, piece], 1, 1
        )
        grad_two = part if grad_two is None else grad_two + part
    g_to[...] = dot(hidden_own.astype(BF), upstream) * scale
    grad_after_cols = upstream.astype(F32) + norm_back(two_f, scale_two, grad_two)
    grad_cols_low = grad_after_cols.astype(BF)

    col_grads = attend_back(
        cq, ck, cv, cgate, cblend, grad_cols_low, co_ref[...], group, col_shares, None
    )
    g_co[...] = dot(dot(own_c, col_gated, 1, 1).astype(BF), grad_cols_low) * scale
    cols_own = dot(own_c, cols_low, 1, 1).astype(BF)
    grad_cols = None
    for f in range(4):
        g_cp[:, f, :] = dot(cols_own, col_grads[f]) * scale
        part = dot(col_grads[f], cp_ref[f], 1, 1)
        grad_cols = part if grad_cols is None else grad_cols + part
    grad_rows_cols = (grad_after_cols + norm_back(cols_f, scale_cols, grad_cols)).astype(BF)

    to_rows_hot = one_hot(
        iota(square, 1)
        == lax.rem(iota(square, 0), residues) * seqs + lax.div(iota(square, 0), residues)
    )
    grad_rows = dot(to_rows_hot, grad_rows_cols).astype(BF)

    bias_shape = (H, H * group)
    at_head, at_row = iota(bias_shape, 0), iota(bias_shape, 1)
    bias_pick = one_hot(
        (lax.div(at_row, group) == at_head) & (lax.rem(at_row, residues) == me)
    )
    bias_sums = []

    def sink(grad_scores, grad_low):
        rest = (grad_scores - grad_low.astype(F32)).astype(BF)
        bias_sums.append(dot(bias_pick, grad_low) + dot(bias_pick, rest))

    row_grads = attend_back(
        rq, rk, rv, rgate, rblend, grad_rows, ro_ref[...], group, row_shares, sink
    )
    bias_sum = bias_sums[0]
    for more in bias_sums[1:]:
        bias_sum = bias_sum + more
    folded = bias_sum[:, 0:residues]
    for at in range(residues, group, residues):
        folded = folded + bias_sum[:, at : at + residues]
    g_bias[:, 0, :] = folded * (residues * seqs ** (-0.5))

    g_ro[...] = dot(dot(own_c, row_gated, 1, 1).astype(BF), grad_rows) * scale
    rows_own = dot(own_c, rows_low, 1, 1).astype(BF)
    own_t = own_rows(me, residues, tokens)
    grad_own = None
    for f in range(4):
        g_rp[:, f, :] = dot(rows_own, row_grads[f]) * scale
        part = dot(dot(own_t, row_grads[f]).astype(BF), rp_ref[f], 1, 1)
        grad_own = part if grad_own is None else grad_own + part
    x_own, scale_own = normalize(x_in[...])
    g_x[...] = (dot(own_t, grad_rows) + norm_back(x_own, scale_own, grad_own)).astype(BF)
    for copy in list(x_copies.values()) + list(ct_copies.values()):
        copy.wait_send()


def hand_over(*refs):
    count = len(refs) // 2
    for i in range(count):
        refs[count + i][...] = refs[i][...]


def whole_shards(
    alignment,
    pair_bias,
    row_project,
    row_output,
    column_project,
    column_output,
    transition_in,
    transition_out,
    cotangent,
):
    nd, nz = lax.axis_size("dap"), lax.axis_size("sub")
    n = nd * nz
    residues = alignment.shape[1]
    tokens = n * residues
    vmem = pl.BlockSpec(memory_space=pltpu.VMEM)
    hbm = pl.BlockSpec(memory_space=pltpu.HBM)
    hidden_units = transition_out.shape[0]
    outs = (
        jax.ShapeDtypeStruct((residues, C), BF),
        jax.ShapeDtypeStruct((H, 1, residues), F32),
        jax.ShapeDtypeStruct((C // n, 4, H * DH), F32),
        jax.ShapeDtypeStruct((H * DH // n, C), F32),
        jax.ShapeDtypeStruct((C // n, 4, H * DH), F32),
        jax.ShapeDtypeStruct((H * DH // n, C), F32),
        jax.ShapeDtypeStruct((C // n, 2, hidden_units), F32),
        jax.ShapeDtypeStruct((hidden_units // n, C), F32),
    )
    weights = (
        row_project,
        row_output,
        column_project,
        column_output,
        transition_in,
        transition_out,
    )
    results = pl.pallas_call(
        functools.partial(sample_body, nd, nz),
        out_shape=outs,
        in_specs=[hbm] * 9,
        out_specs=(vmem,) * 8,
        scratch_shapes=[
            pltpu.VMEM((residues, C), BF),
            pltpu.VMEM((residues, C), BF),
            pltpu.VMEM((H, residues), BF),
            pltpu.VMEM((n, residues, C + LANES), BF),
            pltpu.VMEM((n, residues, C), BF),
        ]
        + [pltpu.VMEM(weight.shape, BF) for weight in weights]
        + [
            pltpu.VMEM((4, C, H * DH), BF),
            pltpu.VMEM((4, C, H * DH), BF),
            pltpu.VMEM((2, C, hidden_units), BF),
            pltpu.VMEM((tokens // LANES, H * LANES, LANES), F32),
            pltpu.VMEM((tokens // LANES, H * LANES, LANES), F32),
            pltpu.SemaphoreType.DMA((len(weights) + 3,)),
        ]
        + [pltpu.SemaphoreType.DMA((nz, nd))] * 4,
        compiler_params=pltpu.CompilerParams(
            collective_id=0, has_side_effects=True, vmem_limit_bytes=63 * 1024 * 1024
        ),
        name="sample_backward",
    )(
        alignment.reshape(residues, C),
        cotangent.reshape(residues, C),
        pair_bias.reshape(H, residues),
        *weights,
    )
    results = pl.pallas_call(
        hand_over,
        out_shape=outs,
        in_specs=[vmem] * len(outs),
        out_specs=(vmem,) * len(outs),
        name="hand_over",
    )(*results)
    return (results[0].reshape(alignment.shape),) + tuple(results[1:])


def shards(alignment, pair_bias, *rest):
    n = lax.axis_size("dap") * lax.axis_size("sub")
    residues = alignment.shape[1]
    tokens = alignment.shape[0] * n * residues
    fits = (
        alignment.shape[0] == 1
        and pair_bias.shape[1] == 1
        and residues >= ROWS
        and residues % ROWS == 0
        and H <= ROWS
        and LANES % residues == 0
        and LANES % n == 0
        and tokens % LANES == 0
        and tokens <= 4 * LANES
    )
    if fits:
        return whole_shards(alignment, pair_bias, *rest)
    return split_shards(alignment, pair_bias, *rest)


def solution(mesh):
    in_specs = (
        P(("grp", "dap", "sub"), None, None),
        P(None, ("grp", "dap", "sub"), None),
        P(),
        P(),
        P(),
        P(),
        P(),
        P(),
        P(("grp", "dap", "sub"), None, None),
    )
    out_specs = (
        P(("grp", "dap", "sub"), None, None),
        P(None, ("grp", "dap", "sub"), None),
        P(("grp", "dap", "sub"), None, None),
        P(("grp", "dap", "sub"), None),
        P(("grp", "dap", "sub"), None, None),
        P(("grp", "dap", "sub"), None),
        P(("grp", "dap", "sub"), None, None),
        P(("grp", "dap", "sub"), None),
    )
    return jax.shard_map(shards, mesh=mesh, in_specs=in_specs, out_specs=out_specs, check_vma=False)
```

```python
import jax
import jax.numpy as jnp
from jax import lax
from jax.experimental import pallas as pl
from jax.experimental.pallas import tpu as pltpu
from jax.sharding import PartitionSpec as P
import functools

C = 256
H = 8
DH = 32


EPSILON = 1e-05


def product(pattern, former, latter):
    return jnp.einsum(pattern, former, latter, preferred_element_type=jnp.float32)


def normalize(values):
    values = values.astype(jnp.float32)
    centred = values - jnp.mean(values, axis=-1, keepdims=True)
    factor = lax.rsqrt(jnp.mean(centred * centred, axis=-1, keepdims=True) + EPSILON)
    return (centred * factor, factor)


def norm_back(normed, factor, upstream):
    mean_up = jnp.mean(upstream, axis=-1, keepdims=True)
    mean_cross = jnp.mean(upstream * normed, axis=-1, keepdims=True)
    return factor * (upstream - mean_up - normed * mean_cross)


def run_items(function, arrays, sequential):
    if sequential:
        return lax.map(lambda bundle: function(*bundle), arrays)
    return jax.vmap(function)(*arrays)


def head_shares(queries, key_rows, bias_head):
    scores = product("qd,kd->qk", queries, key_rows)
    if bias_head is not None:
        scores = scores + bias_head.astype(jnp.float32)
    row_top = jnp.max(scores, axis=-1, keepdims=True)
    powered = jnp.exp(scores - row_top)
    return powered / jnp.sum(powered, axis=-1, keepdims=True)


def head_forward(queries, key_rows, values, bias_head=None):
    shares = head_shares(queries, key_rows, bias_head)
    return product("qk,kd->qd", shares.astype(jnp.bfloat16), values)


def head_backward(queries, key_rows, values, grad_blend, bias_head=None):
    shares = head_shares(queries, key_rows, bias_head)
    shares_low = shares.astype(jnp.bfloat16)
    blended = product("qk,kd->qd", shares_low, values)
    grad_shares = product("qd,kd->qk", grad_blend, values)
    grad_values = product("qk,qd->kd", shares_low, grad_blend)
    centre = jnp.sum(shares * grad_shares, axis=-1, keepdims=True)
    grad_scores = shares * (grad_shares - centre)
    grad_low = grad_scores.astype(jnp.bfloat16)
    grad_queries = product("qk,kd->qd", grad_low, key_rows)
    grad_keys = product("qk,qd->kd", grad_low, queries)
    return (blended, grad_queries, grad_keys, grad_values, grad_scores)


def item_project(normed_item, weights):
    projected = product("lc,cfhd->fhld", normed_item, weights.reshape(C, 4, H, DH))
    queries = (projected[0] * DH ** (-0.5)).astype(jnp.bfloat16)
    key_rows = projected[1].astype(jnp.bfloat16)
    values = projected[2].astype(jnp.bfloat16)
    gating = jax.nn.sigmoid(projected[3])
    return (queries, key_rows, values, gating)


def forward_item(normed_item, weights, bias_table, head_loop):
    queries, key_rows, values, gating = item_project(normed_item, weights)
    if bias_table is None:
        head_args = (queries, key_rows, values)
    else:
        head_args = (queries, key_rows, values, bias_table)
    blended = run_items(head_forward, head_args, head_loop)
    return (blended * gating).astype(jnp.bfloat16)


def backward_item(normed_item, upstream_item, weights, out_weight, bias_table, head_loop):
    queries, key_rows, values, gating = item_project(normed_item, weights)
    grad_gated = product("lc,hdc->hld", upstream_item, out_weight.reshape(H, DH, C))
    grad_blend = (grad_gated * gating).astype(jnp.bfloat16)
    if bias_table is None:
        head_args = (queries, key_rows, values, grad_blend)
    else:
        head_args = (queries, key_rows, values, grad_blend, bias_table)
    blended, grad_queries, grad_keys, grad_values, grad_scores = run_items(
        head_backward, head_args, head_loop
    )
    grad_gate = grad_gated * blended * gating * (1.0 - gating)
    grad_proj = jnp.stack(
        [grad_queries * DH ** (-0.5), grad_keys, grad_values, grad_gate], axis=0
    ).astype(jnp.bfloat16)
    if bias_table is None:
        return (grad_proj, jnp.zeros((), jnp.float32))
    return (grad_proj, grad_scores)


def section_forward(normed_low, weights, bias_table, item_loop, head_loop):

    def single(normed_item):
        return forward_item(normed_item, weights, bias_table, head_loop)

    return run_items(single, (normed_low,), item_loop)


def section_backward(
    normed_low, upstream_low, weights, out_weight, bias_table, item_loop, head_loop
):

    def single(normed_item, upstream_item):
        return backward_item(normed_item, upstream_item, weights, out_weight, bias_table, head_loop)

    if bias_table is None:
        grad_proj, unused = run_items(single, (normed_low, upstream_low), item_loop)
        return (grad_proj, None)

    def accumulate(running, bundle):
        grad_proj, grad_scores = single(bundle[0], bundle[1])
        return (running + grad_scores, grad_proj)

    bias_total, grad_proj = lax.scan(
        accumulate, jnp.zeros(bias_table.shape, jnp.float32), (normed_low, upstream_low)
    )
    return (grad_proj, bias_total)


def column_block(columns, upstream, column_project, column_output, transition_in, transition_out):
    normed_cols, scale_cols = normalize(columns)
    normed_cols_low = normed_cols.astype(jnp.bfloat16)
    column_gated = section_forward(normed_cols_low, column_project, None, False, False)
    column_update = product("bhld,hdc->blc", column_gated, column_output.reshape(H, DH, C))
    after_columns = (columns.astype(jnp.float32) + column_update).astype(jnp.bfloat16)
    normed_two, scale_two = normalize(after_columns)
    normed_two_low = normed_two.astype(jnp.bfloat16)
    pre_hidden = product("blc,cfe->blfe", normed_two_low, transition_in)
    gate_part = pre_hidden[:, :, 0]
    up_part = pre_hidden[:, :, 1]
    sigmoid_gate = jax.nn.sigmoid(gate_part)
    activated = gate_part * sigmoid_gate
    hidden = (activated * up_part).astype(jnp.bfloat16)
    raw_trans_out = product("blf,blc->fc", hidden, upstream)
    grad_hidden = product("blc,fc->blf", upstream, transition_out)
    grad_gate_part = grad_hidden * up_part * sigmoid_gate * (1.0 + gate_part * (1.0 - sigmoid_gate))
    grad_up_part = grad_hidden * activated
    grad_pre = jnp.stack([grad_gate_part, grad_up_part], axis=2).astype(jnp.bfloat16)
    raw_trans_in = product("blc,blfe->cfe", normed_two_low, grad_pre)
    grad_normed_two = product("blfe,cfe->blc", grad_pre, transition_in)
    grad_after_columns = upstream.astype(jnp.float32) + norm_back(
        normed_two, scale_two, grad_normed_two
    )
    grad_columns_low = grad_after_columns.astype(jnp.bfloat16)
    grad_proj, unused = section_backward(
        normed_cols_low, grad_columns_low, column_project, column_output, None, False, False
    )
    raw_column_output = product("bhld,blc->hdc", column_gated, grad_columns_low).reshape(H * DH, C)
    raw_column_project = product("blc,bfhld->cfhd", normed_cols_low, grad_proj).reshape(
        C, 4, H * DH
    )
    grad_normed_cols = product("bfhld,cfhd->blc", grad_proj, column_project.reshape(C, 4, H, DH))
    grad_after_rows = (
        grad_after_columns + norm_back(normed_cols, scale_cols, grad_normed_cols)
    ).astype(jnp.bfloat16)
    return (grad_after_rows, raw_column_project, raw_column_output, raw_trans_in, raw_trans_out)


def row_block(
    normed_rows,
    scale_rows,
    normed_rows_low,
    row_gated,
    grad_after_rows,
    row_project,
    row_output,
    bias_table,
):
    grad_proj, bias_total = section_backward(
        normed_rows_low, grad_after_rows, row_project, row_output, bias_table, True, True
    )
    raw_row_output = product("bhld,blc->hdc", row_gated, grad_after_rows).reshape(H * DH, C)
    raw_row_project = product("blc,bfhld->cfhd", normed_rows_low, grad_proj).reshape(C, 4, H * DH)
    grad_normed_rows = product("bfhld,cfhd->blc", grad_proj, row_project.reshape(C, 4, H, DH))
    grad_alignment = (
        grad_after_rows.astype(jnp.float32) + norm_back(normed_rows, scale_rows, grad_normed_rows)
    ).astype(jnp.bfloat16)
    return (grad_alignment, raw_row_project, raw_row_output, bias_total)


def to_columns(arranged):
    moved = lax.all_to_all(arranged, ("dap", "sub"), split_axis=1, concat_axis=0, tiled=True)
    return moved


def to_rows(arranged):
    moved = lax.all_to_all(arranged, ("dap", "sub"), split_axis=0, concat_axis=1, tiled=True)
    return moved


def split_shards(
    alignment,
    pair_bias,
    row_project,
    row_output,
    column_project,
    column_output,
    transition_in,
    transition_out,
    cotangent,
):
    bias_full = lax.all_gather(pair_bias, ("dap", "sub"), axis=1, tiled=True)
    upstream = jnp.swapaxes(to_columns(cotangent), 0, 1)
    normed_rows, scale_rows = normalize(alignment)
    normed_rows_low = normed_rows.astype(jnp.bfloat16)
    row_gated = section_forward(normed_rows_low, row_project, bias_full, True, True)
    row_update = product("bhld,hdc->blc", row_gated, row_output.reshape(H, DH, C))
    after_rows = (alignment.astype(jnp.float32) + row_update).astype(jnp.bfloat16)
    columns = jnp.swapaxes(to_columns(after_rows), 0, 1)
    grad_columns, raw_column_project, raw_column_output, raw_trans_in, raw_trans_out = column_block(
        columns, upstream, column_project, column_output, transition_in, transition_out
    )
    sequences = alignment.shape[0] * lax.axis_size("dap") * lax.axis_size("sub")
    residues = alignment.shape[1]
    token_scale = (sequences * residues) ** (-0.5)
    term_col_project = raw_column_project * token_scale
    term_col_output = raw_column_output * token_scale
    term_trans_in = raw_trans_in * token_scale
    term_trans_out = raw_trans_out * token_scale
    grad_after_rows = to_rows(jnp.swapaxes(grad_columns, 0, 1))
    grad_alignment, raw_row_project, raw_row_output, bias_total = row_block(
        normed_rows,
        scale_rows,
        normed_rows_low,
        row_gated,
        grad_after_rows,
        row_project,
        row_output,
        bias_full,
    )
    term_row_project = raw_row_project * token_scale
    term_row_output = raw_row_output * token_scale
    bias_term = bias_total * (residues * sequences ** (-0.5))
    grad_bias = lax.psum_scatter(bias_term, ("dap", "sub"), scatter_dimension=1, tiled=True)
    (
        grad_row_project,
        grad_row_output,
        grad_col_project,
        grad_col_output,
        grad_trans_in,
        grad_trans_out,
    ) = (
        lax.psum_scatter(term_row_project, ("dap", "sub"), scatter_dimension=0, tiled=True),
        lax.psum_scatter(term_row_output, ("dap", "sub"), scatter_dimension=0, tiled=True),
        lax.psum_scatter(term_col_project, ("dap", "sub"), scatter_dimension=0, tiled=True),
        lax.psum_scatter(term_col_output, ("dap", "sub"), scatter_dimension=0, tiled=True),
        lax.psum_scatter(term_trans_in, ("dap", "sub"), scatter_dimension=0, tiled=True),
        lax.psum_scatter(term_trans_out, ("dap", "sub"), scatter_dimension=0, tiled=True),
    )
    return (
        grad_alignment,
        grad_bias,
        grad_row_project,
        grad_row_output,
        grad_col_project,
        grad_col_output,
        grad_trans_in,
        grad_trans_out,
    )


LANES = 128
ROWS = 16
BF = jnp.bfloat16
F32 = jnp.float32
MESH = pl.DeviceIdType.MESH


def dot(a, b, left=1, right=0, precision=None):
    return lax.dot_general(
        a, b, (((left,), (right,)), ((), ())), preferred_element_type=F32, precision=precision
    )


def iota(shape, axis):
    return lax.broadcasted_iota(jnp.int32, shape, axis)


def one_hot(condition):
    return jnp.where(condition, 1.0, 0.0).astype(BF)


def own_rows(me, rows, total):
    return one_hot(iota((rows, total), 1) == me * rows + iota((rows, total), 0))


def gang(nd, nz, oz, od):
    d, z = lax.axis_index("dap"), lax.axis_index("sub")
    return lax.rem(d + od, nd), lax.rem(z + oz, nz)


def send(buffer, slot, d, z, send_sem, recv_sem):
    return pltpu.make_async_remote_copy(
        src_ref=buffer.at[slot],
        dst_ref=buffer.at[slot],
        send_sem=send_sem,
        recv_sem=recv_sem,
        device_id={"dap": d, "sub": z},
        device_id_type=MESH,
    )


def spread_own(nd, nz, buffer, send_sem, recv_sem):
    me = lax.axis_index("dap") * nz + lax.axis_index("sub")
    copies = {}
    for oz in range(1, nz):
        d, z = gang(nd, nz, oz, 0)
        copies[oz, 0] = send(buffer, me, d, z, send_sem.at[oz, 0], recv_sem.at[oz, 0])
        copies[oz, 0].start()
    for od in range(1, nd):
        d, z = gang(nd, nz, 0, od)
        copies[0, od] = send(buffer, me, d, z, send_sem.at[0, od], recv_sem.at[0, od])
        copies[0, od].start()
    return copies


def relay(nd, nz, buffer, send_sem, recv_sem, copies):
    for oz in range(1, nz):
        copies[oz, 0].wait_recv()
        from_d, from_z = gang(nd, nz, nz - oz, 0)
        slot = from_d * nz + from_z
        for od in range(1, nd):
            d, z = gang(nd, nz, 0, od)
            copies[oz, od] = send(buffer, slot, d, z, send_sem.at[oz, od], recv_sem.at[oz, od])
            copies[oz, od].start()


def collect(copies):
    for (oz, od), copy in copies.items():
        if od:
            copy.wait_recv()


def head_mask(h, width):
    return one_hot(lax.div(iota((1, width), 1), DH) == h)


def stack_heads(rows):
    width = rows.shape[1]
    return jnp.concatenate([rows * head_mask(h, width) for h in range(H)], axis=0)


def merge_heads(stacked):
    width = stacked.shape[1]
    group = stacked.shape[0] // H
    lane_head = lax.div(iota((1, width), 1), DH)
    total = stacked[0:group]
    for h in range(1, H):
        total = jnp.where(lane_head == h, stacked[h * group : (h + 1) * group], total)
    return total


def block_mask(group, length):
    query = lax.div(lax.rem(iota((H * group, 1), 0), group), length)
    return jnp.where(query == lax.div(iota((1, group), 1), length), 0.0, -1e30)


def project(low, weight_ref):
    parts = [dot(low, weight_ref[f]) for f in range(4)]
    queries = (parts[0] * DH ** (-0.5)).astype(BF)
    return queries, parts[1].astype(BF), parts[2].astype(BF), jax.nn.sigmoid(parts[3])


def attend(queries, keys, values, extra, group, shares_ref):
    blended = []
    for g in range(queries.shape[0] // group):
        rows = slice(g * group, (g + 1) * group)
        scores = dot(stack_heads(queries[rows]), keys[rows], 1, 1) + extra
        powered = jnp.exp(scores - jnp.max(scores, axis=-1, keepdims=True))
        shares = powered * (1.0 / jnp.sum(powered, axis=-1, keepdims=True))
        shares_ref[g] = shares
        blended.append(merge_heads(dot(shares.astype(BF), values[rows])))
    return jnp.concatenate(blended, axis=0)


def attend_back(queries, keys, values, gating, blended, upstream, out_weight, group, shares_ref, score_sink):
    grad_gated = dot(upstream, out_weight, 1, 1)
    grad_blend = (grad_gated * gating).astype(BF)
    grads = ([], [], [])
    for g in range(queries.shape[0] // group):
        rows = slice(g * group, (g + 1) * group)
        shares = shares_ref[g]
        blend_stack = stack_heads(grad_blend[rows])
        grad_shares = dot(blend_stack, values[rows], 1, 1)
        centre = jnp.sum(shares * grad_shares, axis=-1, keepdims=True)
        grad_scores = shares * (grad_shares - centre)
        grad_low = grad_scores.astype(BF)
        if score_sink is not None:
            score_sink(grad_scores, grad_low)
        grads[0].append(merge_heads(dot(grad_low, keys[rows])) * DH ** (-0.5))
        grads[1].append(dot(grad_low, stack_heads(queries[rows]), 0, 0))
        grads[2].append(dot(shares.astype(BF), blend_stack, 0, 0))
    grad_gate = grad_gated * blended * gating * (1.0 - gating)
    parts = [jnp.concatenate(part, axis=0) for part in grads] + [grad_gate]
    return [part.astype(BF) for part in parts]


def sample_body(
    nd,
    nz,
    x_hbm,
    ct_hbm,
    bias_hbm,
    rp_hbm,
    ro_hbm,
    cp_hbm,
    co_hbm,
    ti_hbm,
    to_hbm,
    g_x,
    g_bias,
    g_rp,
    g_ro,
    g_cp,
    g_co,
    g_ti,
    g_to,
    x_in,
    ct_in,
    bias_in,
    x_all,
    ct_all,
    rp_in,
    ro_ref,
    cp_in,
    co_ref,
    ti_in,
    to_ref,
    rp_ref,
    cp_ref,
    ti_ref,
    row_shares,
    col_shares,
    load_sem,
    x_send,
    x_recv,
    ct_send,
    ct_recv,
):
    n = nd * nz
    me = lax.axis_index("dap") * nz + lax.axis_index("sub")
    barrier = pltpu.get_barrier_semaphore()
    for oz in range(nz):
        for od in range(nd):
            if (oz == 0) != (od == 0):
                d, z = gang(nd, nz, oz, od)
                pl.semaphore_signal(
                    barrier, inc=1, device_id={"dap": d, "sub": z}, device_id_type=MESH
                )
    sources = (x_hbm, bias_hbm, ct_hbm, rp_hbm, cp_hbm, ti_hbm, ro_hbm, co_hbm, to_hbm)
    targets = (x_in, bias_in, ct_in, rp_in, cp_in, ti_in, ro_ref, co_ref, to_ref)
    loads = [
        pltpu.make_async_copy(source, target, load_sem.at[i])
        for i, (source, target) in enumerate(zip(sources, targets))
    ]
    for load in loads:
        load.start()
    for load in loads[:3]:
        load.wait()
    loads = loads[3:]
    residues = x_in.shape[0]
    seqs = n
    tokens = seqs * residues
    group = LANES
    scale = tokens ** (-0.5)
    spread = one_hot(lax.rem(iota((residues, LANES), 1), residues) == iota((residues, LANES), 0))
    tiled = dot(bias_in[...], spread)
    padded = jnp.concatenate([tiled, jnp.zeros((ROWS - H, LANES), F32)], axis=0).astype(BF)
    x_all[me, :, 0:C] = x_in[...]
    x_all[me, 0:ROWS, C : C + LANES] = padded
    ct_all[me] = ct_in[...]
    pl.semaphore_wait(barrier, nz + nd - 2)
    x_copies = spread_own(nd, nz, x_all, x_send, x_recv)
    relay(nd, nz, x_all, x_send, x_recv, x_copies)
    ct_copies = spread_own(nd, nz, ct_all, ct_send, ct_recv)
    row_at, col_at = iota((H * group, 1), 0), iota((1, n * ROWS), 1)
    pick = one_hot(lax.rem(row_at, residues) * ROWS + lax.div(row_at, group) == col_at)
    row_mask = block_mask(group, residues)
    col_extra = block_mask(group, seqs)
    token_row, token_col = iota((tokens, 1), 0), iota((1, tokens), 1)
    to_cols = one_hot(
        token_col == lax.rem(token_row, seqs) * residues + lax.div(token_row, seqs)
    )
    to_rows_hot = one_hot(
        token_col == lax.rem(token_row, residues) * seqs + lax.div(token_row, residues)
    )
    loads[0].wait()
    for f in range(4):
        rp_ref[f] = rp_in[:, f, :]
    loads[1].wait()
    for f in range(4):
        cp_ref[f] = cp_in[:, f, :]
    loads[2].wait()
    for f in range(2):
        ti_ref[f] = ti_in[:, f, :]
    for load in loads[3:]:
        load.wait()
    collect(x_copies)

    x = x_all[:, :, 0:C].reshape(tokens, C)
    bias_rows = x_all[:, 0:ROWS, C : C + LANES].reshape(n * ROWS, LANES)

    row_extra = dot(pick, bias_rows) + row_mask

    rows_f, scale_rows = normalize(x)
    rows_low = rows_f.astype(BF)
    rq, rk, rv, rgate = project(rows_low, rp_ref)
    rblend = attend(rq, rk, rv, row_extra, group, row_shares)
    row_gated = (rblend * rgate).astype(BF)
    after_rows = (x.astype(F32) + dot(row_gated, ro_ref[...])).astype(BF)

    relay(nd, nz, ct_all, ct_send, ct_recv, ct_copies)
    columns = dot(to_cols, after_rows).astype(BF)

    cols_f, scale_cols = normalize(columns)
    cols_low = cols_f.astype(BF)
    cq, ck, cv, cgate = project(cols_low, cp_ref)
    cblend = attend(cq, ck, cv, col_extra, group, col_shares)
    col_gated = (cblend * cgate).astype(BF)
    after_cols = (columns.astype(F32) + dot(col_gated, co_ref[...])).astype(BF)

    collect(ct_copies)
    ct = ct_all[...].reshape(tokens, C)
    upstream = dot(to_cols, ct).astype(BF)

    two_f, scale_two = normalize(after_cols)
    two_low = two_f.astype(BF)
    own_c = own_rows(me, C // n, C)
    two_own = dot(own_c, two_low, 1, 1).astype(BF)
    hidden_units = to_ref.shape[0]
    own_f = hidden_units // n
    chunk = C
    grad_two = None
    hidden_own = None
    for at in range(0, hidden_units, chunk):
        piece = slice(at, at + chunk)
        gate_part = dot(two_low, ti_ref[0, :, piece])
        up_part = dot(two_low, ti_ref[1, :, piece])
        sigmoid_gate = jax.nn.sigmoid(gate_part)
        activated = gate_part * sigmoid_gate
        hidden = (activated * up_part).astype(BF)
        select = one_hot(iota((own_f, chunk), 1) + at == me * own_f + iota((own_f, chunk), 0))
        held = dot(select, hidden, 1, 1)
        hidden_own = held if hidden_own is None else hidden_own + held
        grad_hidden = dot(upstream, to_ref[piece, :], 1, 1)
        grad_gate_part = (
            grad_hidden * up_part * sigmoid_gate * (1.0 + gate_part * (1.0 - sigmoid_gate))
        ).astype(BF)
        grad_up_part = (grad_hidden * activated).astype(BF)
        g_ti[:, 0, piece] = dot(two_own, grad_gate_part) * scale
        g_ti[:, 1, piece] = dot(two_own, grad_up_part) * scale
        part = dot(grad_gate_part, ti_ref[0, :, piece], 1, 1) + dot(
            grad_up_part, ti_ref[1, :, piece], 1, 1
        )
        grad_two = part if grad_two is None else grad_two + part
    g_to[...] = dot(hidden_own.astype(BF), upstream) * scale
    grad_after_cols = upstream.astype(F32) + norm_back(two_f, scale_two, grad_two)
    grad_cols_low = grad_after_cols.astype(BF)

    col_grads = attend_back(
        cq, ck, cv, cgate, cblend, grad_cols_low, co_ref[...], group, col_shares, None
    )
    g_co[...] = dot(dot(own_c, col_gated, 1, 1).astype(BF), grad_cols_low) * scale
    cols_own = dot(own_c, cols_low, 1, 1).astype(BF)
    grad_cols = None
    for f in range(4):
        g_cp[:, f, :] = dot(cols_own, col_grads[f]) * scale
        part = dot(col_grads[f], cp_ref[f], 1, 1)
        grad_cols = part if grad_cols is None else grad_cols + part
    grad_rows_cols = (grad_after_cols + norm_back(cols_f, scale_cols, grad_cols)).astype(BF)

    grad_rows = dot(to_rows_hot, grad_rows_cols).astype(BF)

    bias_shape = (H, H * group)
    at_head, at_row = iota(bias_shape, 0), iota(bias_shape, 1)
    bias_pick = one_hot(
        (lax.div(at_row, group) == at_head) & (lax.rem(at_row, residues) == me)
    )
    bias_sums = []

    def sink(grad_scores, grad_low):
        rest = (grad_scores - grad_low.astype(F32)).astype(BF)
        bias_sums.append(dot(bias_pick, grad_low) + dot(bias_pick, rest))

    row_grads = attend_back(
        rq, rk, rv, rgate, rblend, grad_rows, ro_ref[...], group, row_shares, sink
    )
    bias_sum = bias_sums[0]
    for more in bias_sums[1:]:
        bias_sum = bias_sum + more
    folded = bias_sum[:, 0:residues]
    for at in range(residues, group, residues):
        folded = folded + bias_sum[:, at : at + residues]
    g_bias[:, 0, :] = folded * (residues * seqs ** (-0.5))

    g_ro[...] = dot(dot(own_c, row_gated, 1, 1).astype(BF), grad_rows) * scale
    rows_own = dot(own_c, rows_low, 1, 1).astype(BF)
    own_t = own_rows(me, residues, tokens)
    grad_own = None
    for f in range(4):
        g_rp[:, f, :] = dot(rows_own, row_grads[f]) * scale
        part = dot(dot(own_t, row_grads[f]).astype(BF), rp_ref[f], 1, 1)
        grad_own = part if grad_own is None else grad_own + part
    x_own, scale_own = normalize(x_in[...])
    g_x[...] = (dot(own_t, grad_rows) + norm_back(x_own, scale_own, grad_own)).astype(BF)
    for copy in list(x_copies.values()) + list(ct_copies.values()):
        copy.wait_send()


def hand_over(*refs):
    count = len(refs) // 2
    for i in range(count):
        refs[count + i][...] = refs[i][...]


def whole_shards(
    alignment,
    pair_bias,
    row_project,
    row_output,
    column_project,
    column_output,
    transition_in,
    transition_out,
    cotangent,
):
    nd, nz = lax.axis_size("dap"), lax.axis_size("sub")
    n = nd * nz
    residues = alignment.shape[1]
    tokens = n * residues
    vmem = pl.BlockSpec(memory_space=pltpu.VMEM)
    hbm = pl.BlockSpec(memory_space=pltpu.HBM)
    hidden_units = transition_out.shape[0]
    outs = (
        jax.ShapeDtypeStruct((residues, C), BF),
        jax.ShapeDtypeStruct((H, 1, residues), F32),
        jax.ShapeDtypeStruct((C // n, 4, H * DH), F32),
        jax.ShapeDtypeStruct((H * DH // n, C), F32),
        jax.ShapeDtypeStruct((C // n, 4, H * DH), F32),
        jax.ShapeDtypeStruct((H * DH // n, C), F32),
        jax.ShapeDtypeStruct((C // n, 2, hidden_units), F32),
        jax.ShapeDtypeStruct((hidden_units // n, C), F32),
    )
    weights = (
        row_project,
        row_output,
        column_project,
        column_output,
        transition_in,
        transition_out,
    )
    results = pl.pallas_call(
        functools.partial(sample_body, nd, nz),
        out_shape=outs,
        in_specs=[hbm] * 9,
        out_specs=(vmem,) * 8,
        scratch_shapes=[
            pltpu.VMEM((residues, C), BF),
            pltpu.VMEM((residues, C), BF),
            pltpu.VMEM((H, residues), BF),
            pltpu.VMEM((n, residues, C + LANES), BF),
            pltpu.VMEM((n, residues, C), BF),
        ]
        + [pltpu.VMEM(weight.shape, BF) for weight in weights]
        + [
            pltpu.VMEM((4, C, H * DH), BF),
            pltpu.VMEM((4, C, H * DH), BF),
            pltpu.VMEM((2, C, hidden_units), BF),
            pltpu.VMEM((tokens // LANES, H * LANES, LANES), F32),
            pltpu.VMEM((tokens // LANES, H * LANES, LANES), F32),
            pltpu.SemaphoreType.DMA((len(weights) + 3,)),
        ]
        + [pltpu.SemaphoreType.DMA((nz, nd))] * 4,
        compiler_params=pltpu.CompilerParams(
            collective_id=0, has_side_effects=True, vmem_limit_bytes=63 * 1024 * 1024
        ),
        name="sample_backward",
    )(
        alignment.reshape(residues, C),
        cotangent.reshape(residues, C),
        pair_bias.reshape(H, residues),
        *weights,
    )
    results = pl.pallas_call(
        hand_over,
        out_shape=outs,
        in_specs=[vmem] * len(outs),
        out_specs=(vmem,) * len(outs),
        name="hand_over",
    )(*results)
    return (results[0].reshape(alignment.shape),) + tuple(results[1:])


def shards(alignment, pair_bias, *rest):
    n = lax.axis_size("dap") * lax.axis_size("sub")
    residues = alignment.shape[1]
    tokens = alignment.shape[0] * n * residues
    fits = (
        alignment.shape[0] == 1
        and pair_bias.shape[1] == 1
        and residues >= ROWS
        and residues % ROWS == 0
        and H <= ROWS
        and LANES % residues == 0
        and LANES % n == 0
        and tokens % LANES == 0
        and tokens <= 4 * LANES
    )
    if fits:
        return whole_shards(alignment, pair_bias, *rest)
    return split_shards(alignment, pair_bias, *rest)


def solution(mesh):
    in_specs = (
        P(("grp", "dap", "sub"), None, None),
        P(None, ("grp", "dap", "sub"), None),
        P(),
        P(),
        P(),
        P(),
        P(),
        P(),
        P(("grp", "dap", "sub"), None, None),
    )
    out_specs = (
        P(("grp", "dap", "sub"), None, None),
        P(None, ("grp", "dap", "sub"), None),
        P(("grp", "dap", "sub"), None, None),
        P(("grp", "dap", "sub"), None),
        P(("grp", "dap", "sub"), None, None),
        P(("grp", "dap", "sub"), None),
        P(("grp", "dap", "sub"), None, None),
        P(("grp", "dap", "sub"), None),
    )
    return jax.shard_map(shards, mesh=mesh, in_specs=in_specs, out_specs=out_specs, check_vma=False)
```
